512 devices in a mesh: slab: 16 (over x, y_hi), mode: 32 (over z, y_lo, core).
Axes of the slice: x: 4, y: 8 (y_hi: 4, y_lo: 2; y = y_hi * 2 + y_lo), z: 8, core: 2. Of those that a mesh axis runs over, the one named last changes fastest.
Arguments:
- log_coeffs: bfloat16 [192, 16, 128, 128], P('mode', 'slab'), may hold values from -0.23925781 to 0.23925781
- pressure: bfloat16 [192, 16, 128, 128], P('mode', 'slab'), may hold values from -0.41992188 to 0.41992188
- source: bfloat16 [192, 16, 128, 128], P('mode', 'slab'), may hold values from -6 to 6
- vandermonde: float32 [512, 192], replicated, may hold values from -4 to 4
- weights: float32 [512], replicated, may hold values from 0.02 to 0.2
Outputs:
- residual: bfloat16 [192, 16, 128, 128], P('mode', 'slab')
The draws below stay inside these ranges and needn't reach their ends.
All inputs are finite; a program needn't handle non-finite values.
Results may differ from the reference program's by a relative error of at most 0.005.
Values may be sent and summed in bfloat16 or wider, within the bound.
No kernel may reach another device: no remote copies, remote signals or barrier semaphores. Data moves between devices by JAX's collectives and lax.ppermute only.
A program may use at most 64 MiB of HBM per device.

```python
import math
import jax
import jax.numpy as jnp
from jax import lax

M = 192
Q = 512
NX = 128
NY = 128
NZ = 16


def block_levels(own_key, dims, pieces, smallest, top_value):
    factor_of = 1.0
    for position, shards_of in pieces:
        heights = jax.random.uniform(jax.random.fold_in(jax.random.fold_in(own_key, 6), position), (shards_of,), jnp.float32, smallest / len(pieces), top_value / len(pieces))
        factor_of = factor_of * jnp.repeat(jnp.exp(heights), dims[position] // shards_of).reshape((-1,) + (1,) * (len(dims) - 1 - position))
    return factor_of


def bell_draw(stream_key, shape, scale, reach, split=(), kind=jnp.bfloat16):
    values = jax.random.normal(stream_key, shape, jnp.float32) * scale
    if len(split) > 0:
        values = block_levels(stream_key, shape, split, -0.22, 0.18) * values
    return jnp.clip(values, min=-reach, max=reach).astype(kind)


def setup_inputs(seed: int = 0) -> dict:
    seeds = jax.random.split(jax.random.key(seed), 6)
    return {
        "log_coeffs": bell_draw(seeds[0], (M, NZ, NY, NX), 0.04, 0.23925781, ((0, 32), (1, 16))),
        "pressure": bell_draw(seeds[1], (M, NZ, NY, NX), 0.07, 0.41992188, ((0, 32), (1, 16))),
        "source": bell_draw(seeds[2], (M, NZ, NY, NX), 1.0, 6.0, ((0, 32), (1, 16))),
        "vandermonde": bell_draw(seeds[3], (Q, M), 1.0, 4.0, (), jnp.float32),
        "weights": jnp.clip(jnp.exp(jax.random.uniform(seeds[4], (Q,), jnp.float32, math.log(0.02), math.log(0.2))), 0.02, 0.2),
    }


def reference(log_coeffs, pressure, source, vandermonde, weights):
    projector = jnp.transpose(vandermonde * weights[:, None])

    def apply_matrix(matrix, field):
        flat = field.reshape(field.shape[0], -1)
        return jnp.dot(matrix, flat, precision=lax.Precision.HIGHEST, preferred_element_type=jnp.float32)

    def plane_terms(index):
        upper = (index + 1) % NZ
        coeffs = lax.dynamic_index_in_dim(log_coeffs, index, 1, keepdims=False).astype(jnp.float32)
        here = lax.dynamic_index_in_dim(pressure, index, 1, keepdims=False).astype(jnp.float32)
        above = lax.dynamic_index_in_dim(pressure, upper, 1, keepdims=False).astype(jnp.float32)
        slope_x = jnp.roll(here, -1, axis=2) - here
        slope_y = jnp.roll(here, -1, axis=1) - here
        slope_z = above - here
        factor = jnp.exp(apply_matrix(vandermonde, coeffs))
        results = []
        for slope in (slope_x, slope_y, slope_z):
            flux = factor * apply_matrix(vandermonde, slope)
            results.append(apply_matrix(projector, flux).reshape(here.shape))
        proj_x, proj_y, proj_z = results
        local = (proj_x - jnp.roll(proj_x, 1, axis=2)) + (proj_y - jnp.roll(proj_y, 1, axis=1))
        return local, proj_z

    locals_all, upward = lax.map(plane_terms, jnp.arange(NZ, dtype=jnp.int32))
    spread = locals_all + (upward - jnp.roll(upward, 1, axis=0))
    spread = jnp.transpose(spread, (1, 0, 2, 3))
    return (-spread - source.astype(jnp.float32)).astype(jnp.bfloat16)
```

```python
import functools

import jax
import jax.numpy as jnp
from jax import lax
from jax.experimental import pallas as pl
from jax.experimental.pallas import tpu as pltpu
from jax.sharding import PartitionSpec as P

F32 = jnp.float32
BF16 = jnp.bfloat16
OWN = 6
GROUP = 32
ROWS = 4
M = OWN * GROUP
Q = 512
X = 128
CELLS = ROWS * X
VMEM = 48 * 1024 * 1024


def slab_shift(block, distance):
    devices = range(lax.axis_size("slab"))
    route = [((i - distance) % len(devices), i) for i in devices]
    return lax.ppermute(block, "slab", route)


def exchange(block):
    return lax.all_to_all(block, "mode", split_axis=0, concat_axis=0, tiled=True)


def halves(values):
    high = values.astype(BF16)
    return high, (values - high.astype(F32)).astype(BF16)


def dot(a, b):
    return jnp.dot(a, b, preferred_element_type=F32)


def pack_kernel(log_ref, pressure_ref, out_ref, wide, block):
    for offset, ref in ((0, log_ref), (24, pressure_ref)):
        for m in range(OWN):
            wide[...] = ref[m].astype(F32).reshape(16, 8, X)
            at = offset + m * ROWS
            block[:, 0, at : at + ROWS, :] = wide[:, 0:4, :]
            block[:, 1, at : at + ROWS, :] = wide[:, 4:8, :]
            if offset:
                block[:, 0, 48 + m, :] = wide[:, 4, :]
                block[0:15, 1, 48 + m, :] = wide[1:16, 0, :]
                block[15:16, 1, 48 + m, :] = wide[0:1, 0, :]
    block[:, :, 54:56, :] = jnp.zeros((16, 2, 2, X), F32)
    out_ref[...] = block[...].astype(BF16)


def by_rows(rows, flat, out_ref):
    flat[...] = rows.reshape(M * ROWS, X)
    for j in range(ROWS):
        out_ref[:, j * X : (j + 1) * X] = flat[pl.ds(j, M, stride=ROWS), :].astype(BF16)


def own_kernel(
    got_ref, vander_ref, weights_ref,
    vh_ref, vl_ref, ph_ref, pl_ref, factor_ref, field_ref, local_ref, edge_ref,
    wide, flat, halo, logs, press, fields,
):
    vh, vl = halves(vander_ref[...])
    vh_ref[...] = vh
    vl_ref[...] = vl
    ph, plow = halves(jnp.transpose(vander_ref[...] * weights_ref[...]))
    ph_ref[...] = ph
    pl_ref[...] = plow
    wide[...] = got_ref[...].astype(F32)
    by_rows(wide[:, 0:24, :], flat, logs)
    by_rows(wide[:, 24:48, :], flat, press)
    for owner in range(GROUP):
        halo[owner * OWN : (owner + 1) * OWN, :] = wide[owner, 48 : 48 + OWN, :]
    press[:, CELLS : CELLS + X] = halo[...].astype(BF16)
    factor_ref[...] = jnp.exp(dot(vh_ref[...], logs[...]) + dot(vl_ref[...], logs[...]))
    fields[...] = dot(vh_ref[...], press[...]) + dot(vl_ref[...], press[...])
    field_ref[...] = fields[:, 0:CELLS]
    before = None
    for j in range(ROWS):
        here = fields[:, j * X : (j + 1) * X]
        factor = factor_ref[:, j * X : (j + 1) * X]
        flux_x = factor * (pltpu.roll(here, X - 1, 1) - here)
        flux_y = factor * (fields[:, (j + 1) * X : (j + 2) * X] - here)
        total = flux_x - pltpu.roll(flux_x, 1, 1) + flux_y
        if before is not None:
            total = total - before
        local_ref[:, j * X : (j + 1) * X] = total
        before = flux_y
    fh, fl = halves(before)
    edge_ref[...] = dot(ph_ref[...], fh) + dot(pl_ref[...], fh) + dot(ph_ref[...], fl)


def join_kernel(
    upper_ref, lower_ref, vh_ref, vl_ref, ph_ref, pl_ref, factor_ref, field_ref, local_ref, edge_ref,
    out_ref,
    wide, flat, logs, press, block,
):
    by_rows(upper_ref[...].astype(F32), flat, press)
    rise = dot(vh_ref[...], press[...]) + dot(vl_ref[...], press[...]) - field_ref[...]
    total = local_ref[...] + factor_ref[...] * rise
    wide[...] = lower_ref[...].astype(F32)
    by_rows(wide[:, 0:24, :], flat, logs)
    by_rows(wide[:, 24:48, :], flat, press)
    factor = jnp.exp(dot(vh_ref[...], logs[...]) + dot(vl_ref[...], logs[...]))
    rise = field_ref[...] - (dot(vh_ref[...], press[...]) + dot(vl_ref[...], press[...]))
    fh, fl = halves(total - factor * rise)
    spread = dot(ph_ref[...], fh) + dot(pl_ref[...], fh) + dot(ph_ref[...], fl)
    for j in range(ROWS):
        flat[pl.ds(j, M, stride=ROWS), :] = spread[:, j * X : (j + 1) * X]
    block[:, 0:24, :] = flat[...].reshape(GROUP, 24, X)
    for owner in range(GROUP):
        block[owner, 24 : 24 + OWN, :] = edge_ref[owner * OWN : (owner + 1) * OWN, :]
    block[:, 30:32, :] = jnp.zeros((GROUP, 2, X), F32)
    out_ref[...] = block[...].astype(BF16)


def finish_kernel(got_ref, source_ref, out_ref, wide, plane):
    wide[...] = got_ref[...].astype(F32)
    for m in range(OWN):
        at = m * ROWS
        plane[:, 0:4, :] = wide[:, 0, at : at + ROWS, :]
        plane[:, 4:8, :] = wide[:, 1, at : at + ROWS, :]
        plane[0:1, 0, :] -= wide[15:16, 1, 24 + m, :]
        plane[1:16, 0, :] -= wide[0:15, 1, 24 + m, :]
        plane[:, 4, :] -= wide[:, 0, 24 + m, :]
        out_ref[m] = (-plane[...].reshape(X, X) - source_ref[m].astype(F32)).astype(BF16)


def call(kernel, outs, scratch, cost):
    outs = [jax.ShapeDtypeStruct(shape, dtype) for shape, dtype in outs]
    return pl.pallas_call(
        kernel,
        out_shape=outs if len(outs) > 1 else outs[0],
        scratch_shapes=[pltpu.VMEM(shape, dtype) for shape, dtype in scratch],
        compiler_params=pltpu.CompilerParams(vmem_limit_bytes=VMEM),
        cost_estimate=pl.CostEstimate(flops=cost, bytes_accessed=2**20, transcendentals=0),
    )


def shards(log_coeffs, pressure, source, vandermonde, weights):
    plane = (OWN, X, X)
    packed = call(
        pack_kernel,
        [((16, 2, 56, X), BF16)],
        [((16, 8, X), F32), ((16, 2, 56, X), F32)],
        10**6,
    )(log_coeffs.reshape(plane), pressure.reshape(plane))
    got = exchange(packed.reshape(GROUP, 56, X))
    upper = slab_shift(got[:, 24:48], -1)
    lower = slab_shift(got[:, 0:48], 1)
    own = call(
        own_kernel,
        [
            ((Q, M), BF16), ((Q, M), BF16), ((M, Q), BF16), ((M, Q), BF16),
            ((Q, CELLS), F32), ((Q, CELLS), F32), ((Q, CELLS), F32), ((M, X), F32),
        ],
        [
            ((GROUP, 56, X), F32), ((M * ROWS, X), F32), ((M, X), F32),
            ((M, CELLS), BF16), ((M, CELLS + X), BF16), ((Q, CELLS + X), F32),
        ],
        10**9,
    )(got, vandermonde, weights.reshape(Q, 1))
    back = call(
        join_kernel,
        [((GROUP, 32, X), BF16)],
        [
            ((GROUP, 48, X), F32), ((M * ROWS, X), F32),
            ((M, CELLS), BF16), ((M, CELLS), BF16), ((GROUP, 32, X), F32),
        ],
        10**9,
    )(upper, lower, *own)
    returned = exchange(back)
    result = call(
        finish_kernel,
        [(plane, BF16)],
        [((16, 2, 32, X), F32), ((16, 8, X), F32)],
        10**6,
    )(returned.reshape(16, 2, 32, X), source.reshape(plane))
    return result.reshape(OWN, 1, X, X)


def solution(mesh):
    placed = (
        P("mode", "slab", None, None),
        P("mode", "slab", None, None),
        P("mode", "slab", None, None),
        P(),
        P(),
    )
    return jax.shard_map(
        shards, mesh=mesh, in_specs=placed, out_specs=P("mode", "slab", None, None), check_vma=False
    )
```

```python
import jax
import jax.numpy as jnp
from jax import lax
from jax.experimental import pallas as pl
from jax.experimental.pallas import tpu as pltpu
from jax.sharding import Mesh
from jax.sharding import PartitionSpec as P

F32 = jnp.float32
BF16 = jnp.bfloat16
OWN = 6
OWNERS = 32
M = OWN * OWNERS
Q = 512
X = 128
PLANES = 4
ROWS = 4
COLS = 32
ACROSS = 4
DOWN = 32
CELLS = PLANES * X
SENT = 14
VMEM = 48 * 1024 * 1024


def halves(values):
    high = values.astype(BF16)
    return high, (values - high.astype(F32)).astype(BF16)


def dot(a, b):
    return jnp.dot(a, b, preferred_element_type=F32)


def expand(vh_ref, vl_ref, field):
    return dot(vh_ref[...], field) + dot(vl_ref[...], field)


def project(ph_ref, pl_ref, flux):
    fh, fl = halves(flux)
    return dot(ph_ref[...], fh) + dot(pl_ref[...], fh) + dot(ph_ref[...], fl)


def lane_of(rows):
    return lax.broadcasted_iota(jnp.int32, (rows, X), 1)


def turn(values, lanes):
    lanes = lanes % X
    return pltpu.roll(values, lanes, 1) if lanes else values


def grid_of(rows, columns):
    return tuple(lax.broadcasted_iota(jnp.int32, (rows, columns), axis) for axis in (0, 1))


def select(flags):
    return flags.astype(F32).astype(BF16)


def swapper():
    row, col = grid_of(4 * X, 4 * X)
    return select(row == col % X // COLS * X + col // X * COLS + col % COLS)


def start_all(copies):
    for copy in copies:
        copy.start()
    return copies


def pack_kernel(log_any, pressure_any, out_ref, planes, flat, ring, swap, shift, cells, heads, block, sems):
    copies = start_all([
        pltpu.make_async_copy(ref.at[m], planes.at[field, m], sems.at[field, m])
        for field, ref in enumerate((log_any, pressure_any))
        for m in range(OWN)
    ])
    swap[...] = swapper()
    row, col = grid_of(X, X)
    for m in range(OWN):
        shift[m * X : (m + 1) * X, :] = select((col % COLS == 26 + m) & (row == col - 26 - m))
    for field in range(2):
        for m in range(OWN):
            copies[field * OWN + m].wait()
            flat[...] = planes[field, m].astype(F32)
            rows = slice((field * OWN + m) * DOWN, (field * OWN + m + 1) * DOWN)
            for j in range(ROWS):
                cells[rows, j * X : (j + 1) * X] = flat[pl.ds(j, DOWN, stride=ROWS), :].astype(BF16)
            if field:
                ring[0:DOWN, :] = flat[pl.ds(0, DOWN, stride=ROWS), :]
                ring[DOWN : DOWN + 1, :] = flat[0:1, :]
                after = ring[1 : DOWN + 1, :]
                if m < 4:
                    cells[2 * M : 2 * M + DOWN, m * X : (m + 1) * X] = after.astype(BF16)
                else:
                    at = 2 * (m - 4) * X
                    cells[2 * M + DOWN :, at : at + X] = after.astype(BF16)
                    cells[2 * M + DOWN :, at + X : at + 2 * X] = turn(after, -16).astype(BF16)
    swapped = dot(cells[...], swap[...])
    for b in range(ACROSS):
        start = SENT * DOWN * b
        for field, offset in enumerate((0, 8)):
            for m in range(OWN):
                rows = slice((field * OWN + m) * DOWN, (field * OWN + m + 1) * DOWN)
                total = swapped[rows, b * X : (b + 1) * X]
                block[pl.ds(start + offset + m, DOWN, stride=SENT), :] = total
                if field:
                    left = (b - 1) % ACROSS
                    heads[left * DOWN : (left + 1) * DOWN, m * X : (m + 1) * X] = total.astype(BF16)
        block[pl.ds(start + 6, DOWN, stride=SENT), :] = swapped[2 * M : 2 * M + DOWN, b * X : (b + 1) * X]
    rights = dot(heads[...], shift[...])
    within = lane_of(DOWN) % COLS
    for b in range(ACROSS):
        ends = swapped[2 * M + DOWN :, b * X : (b + 1) * X]
        total = jnp.where(within < 16, ends, rights[b * DOWN : (b + 1) * DOWN])
        block[pl.ds(SENT * DOWN * b + 7, DOWN, stride=SENT), :] = total
    out_ref[...] = block[...].astype(BF16)


def own_kernel(
    got_ref, vander_ref, weights_ref,
    vh_ref, vl_ref, ph_ref, pl_ref, factor_ref, field_ref, block_ref,
    wide, turned, ordered, logs, press, right, below, cells, ends, edges, columns,
):
    for c in range(Q // X):
        points = slice(c * X, (c + 1) * X)
        turned[...] = jnp.transpose(vander_ref[points, :])
        for m in range(OWN):
            ordered[m * OWNERS : (m + 1) * OWNERS, points] = turned[pl.ds(m, OWNERS, stride=OWN), :]
    vh_ref[...], vl_ref[...] = halves(jnp.transpose(ordered[...]))
    ph_ref[...], pl_ref[...] = halves(ordered[...] * weights_ref[...])
    row, col = grid_of(X, X)
    within = col % COLS
    for m in range(4):
        columns[:, m * X : (m + 1) * X] = select((col >= 96) & (row == col - 96 + COLS * m))
    for m in range(OWN):
        at = (4 + m) * X
        columns[:, at : at + X] = select((within == COLS - 1) & (row == col - 5 + m))
    for m in range(4, OWN):
        at = (6 + m) * X
        half = jnp.where(col >= 112, 80, 96)
        columns[:, at : at + X] = select((col >= 96) & (row == col - half + 64 * (m - 4)))
    wide[...] = got_ref[...].astype(F32)
    for k in range(PLANES):
        lanes = slice(k * X, (k + 1) * X)
        for r in range(2):
            ends[r, k * OWNERS : (k + 1) * OWNERS, :] = wide[
                pl.ds(SENT * OWNERS * k + 6 + r, OWNERS, stride=SENT), :
            ].astype(BF16)
        for m in range(OWN):
            modes = slice(m * OWNERS, (m + 1) * OWNERS)
            logs[modes, lanes] = wide[pl.ds(SENT * OWNERS * k + m, OWNERS, stride=SENT), :].astype(BF16)
            here = wide[pl.ds(SENT * OWNERS * k + 8 + m, OWNERS, stride=SENT), :].astype(BF16)
            press[modes, lanes] = here
            cells[k * M + m * OWNERS : k * M + (m + 1) * OWNERS, :] = here
    next_x = dot(cells[...], select((within < COLS - 1) & (row == col + 1)))
    next_y = dot(cells[...], select(row == col + COLS))
    past_y = dot(ends[0], columns[:, 0 : 4 * X])
    past = dot(ends[1], columns[:, 4 * X :])
    for k in range(PLANES):
        lanes = slice(k * X, (k + 1) * X)
        owners = slice(k * OWNERS, (k + 1) * OWNERS)
        for m in range(OWN):
            modes = slice(m * OWNERS, (m + 1) * OWNERS)
            rows = slice(k * M + m * OWNERS, k * M + (m + 1) * OWNERS)
            right[modes, lanes] = (next_x[rows] + past[owners, m * X : (m + 1) * X]).astype(BF16)
            if m < 4:
                after = past_y[owners, m * X : (m + 1) * X]
            else:
                after = past[owners, (m + 2) * X : (m + 3) * X]
            below[modes, lanes] = (next_y[rows] + after).astype(BF16)
    factor_ref[...] = jnp.exp(expand(vh_ref, vl_ref, logs[...]))
    field_ref[...] = expand(vh_ref, vl_ref, press[...])
    flux_x = factor_ref[...] * (expand(vh_ref, vl_ref, right[...]) - field_ref[...])
    proj_x = project(ph_ref, pl_ref, flux_x)
    flux_y = factor_ref[...] * (expand(vh_ref, vl_ref, below[...]) - field_ref[...])
    proj_y = project(ph_ref, pl_ref, flux_y)
    inner = CELLS - X
    flux_z = factor_ref[:, 0:inner] * (field_ref[:, X:CELLS] - field_ref[:, 0:inner])
    proj_z = project(ph_ref, pl_ref, flux_z)
    xh, xl = halves(proj_x)
    yh, yl = halves(proj_y)
    less_x = (row == col).astype(F32) - ((within > 0) & (row == col - 1)).astype(F32)
    less_x = less_x.astype(BF16)
    less_y = ((row == col).astype(F32) - (row == col - COLS).astype(F32)).astype(BF16)
    for k in range(PLANES):
        lanes = slice(k * X, (k + 1) * X)
        owners = slice(k * OWNERS, (k + 1) * OWNERS)
        total = dot(xh[:, lanes], less_x) + dot(xl[:, lanes], less_x)
        total = total + dot(yh[:, lanes], less_y) + dot(yl[:, lanes], less_y)
        if k < PLANES - 1:
            total = total + proj_z[:, lanes]
        if k > 0:
            total = total - proj_z[:, (k - 1) * X : k * X]
        for m in range(OWN):
            modes = slice(m * OWNERS, (m + 1) * OWNERS)
            block_ref[owners, m, :] = total[modes]
            at = (m if m < 4 else 6 + m) * X
            edges[owners, at : at + X] = yh[modes, lanes]
            edges[owners, (4 + m) * X : (5 + m) * X] = xh[modes, lanes]
    back = (((1,), (1,)), ((), ()))
    block_ref[:, 6, :] = lax.dot_general(
        edges[:, 0 : 4 * X], columns[:, 0 : 4 * X], back, preferred_element_type=F32
    )
    block_ref[:, 7, :] = lax.dot_general(
        edges[:, 4 * X :], columns[:, 4 * X :], back, preferred_element_type=F32
    )


def join_kernel(
    upper_ref, lower_ref, vh_ref, vl_ref, ph_ref, pl_ref, factor_ref, field_ref, block_ref,
    out_ref,
    wide, above, faces, block,
):
    above[...] = upper_ref[...].astype(F32)
    wide[...] = lower_ref[...].astype(F32)
    for m in range(OWN):
        modes = slice(m * OWNERS, (m + 1) * OWNERS)
        faces[modes, 0:X] = above[pl.ds(m, OWNERS, stride=OWN), :].astype(BF16)
        faces[modes, X : 2 * X] = wide[pl.ds(m, OWNERS, stride=SENT), :].astype(BF16)
        faces[modes, 2 * X : 3 * X] = wide[pl.ds(8 + m, OWNERS, stride=SENT), :].astype(BF16)
    last = slice(CELLS - X, CELLS)
    values = expand(vh_ref, vl_ref, faces[...])
    top = factor_ref[:, last] * (values[:, 0:X] - field_ref[:, last])
    bottom = jnp.exp(values[:, X : 2 * X]) * (field_ref[:, 0:X] - values[:, 2 * X : 3 * X])
    both = project(ph_ref, pl_ref, jnp.concatenate([bottom, top], axis=1))
    block[...] = block_ref[...]
    for m in range(OWN):
        modes = slice(m * OWNERS, (m + 1) * OWNERS)
        block[0:OWNERS, m, :] -= both[modes, 0:X]
        block[3 * OWNERS : 4 * OWNERS, m, :] += both[modes, X : 2 * X]
    out_ref[...] = block[...].astype(BF16)


def finish_kernel(got_ref, source_ref, out_any, wide, ring, swap, shift, cells, ends, flat, planes, sems):
    swap[...] = swapper()
    row, col = grid_of(X, X)
    within = col % COLS
    for m in range(OWN):
        here = select((within == 0) & (row == (col + X - COLS) % X + 26 + m))
        shift[:, m * X : (m + 1) * X] = here
    wide[...] = got_ref[...].astype(F32)
    for b in range(ACROSS):
        lanes = slice(b * X, (b + 1) * X)
        for m in range(OWN):
            cells[m * DOWN : (m + 1) * DOWN, lanes] = wide[b, :, m, :].astype(BF16)
        cells[M : M + DOWN, lanes] = wide[b, :, 7, :].astype(BF16)
        for r in range(2):
            ring[1 : DOWN + 1, :] = wide[b, :, 6 + r, :]
            ring[0:1, :] = wide[b, DOWN - 1 : DOWN, 6 + r, :]
            at = M + (1 + r) * DOWN
            cells[at : at + DOWN, lanes] = ring[0:DOWN, :].astype(BF16)
    swapped = dot(cells[...], swap[...])
    for j in range(ROWS):
        ends[j * DOWN : (j + 1) * DOWN, :] = swapped[M : M + DOWN, j * X : (j + 1) * X].astype(BF16)
    beside = dot(ends[...], shift[...])
    above = swapped[M + DOWN : M + 2 * DOWN]
    halved = swapped[M + 2 * DOWN :]
    inside = lane_of(DOWN) % COLS < 16
    copies = []
    for m in range(OWN):
        modes = slice(m * DOWN, (m + 1) * DOWN)
        for j in range(ROWS):
            total = swapped[modes, j * X : (j + 1) * X]
            total = total - beside[j * DOWN : (j + 1) * DOWN, m * X : (m + 1) * X]
            if j == 0 and m < 4:
                total = total - above[:, m * X : (m + 1) * X]
            elif j == 0:
                at = 2 * (m - 4) * X
                far = turn(halved[:, at + X : at + 2 * X], 16)
                total = total - jnp.where(inside, halved[:, at : at + X], far)
            flat[pl.ds(j, DOWN, stride=ROWS), :] = total
        planes[m] = (-flat[...] - source_ref[m].astype(F32)).astype(BF16)
        copies.append(pltpu.make_async_copy(planes.at[m], out_any.at[m], sems.at[m]))
        copies[m].start()
    for copy in copies:
        copy.wait()


def call(kernel, outs, scratch, cost, **rest):
    outs = [jax.ShapeDtypeStruct(shape, dtype) for shape, dtype in outs]
    scratch = [pltpu.VMEM(*entry) if isinstance(entry, tuple) else entry for entry in scratch]
    return pl.pallas_call(
        kernel,
        out_shape=outs if len(outs) > 1 else outs[0],
        scratch_shapes=scratch,
        compiler_params=pltpu.CompilerParams(vmem_limit_bytes=VMEM),
        cost_estimate=pl.CostEstimate(flops=cost, bytes_accessed=2**20, transcendentals=0),
        **rest,
    )


def neighbour(block, distance):
    devices = range(lax.axis_size("x"))
    route = [((i - distance) % len(devices), i) for i in devices]
    return lax.ppermute(block, "x", route)


def exchange(block):
    return lax.all_to_all(block, ("y", "mode"), split_axis=0, concat_axis=0, tiled=True)


def shards(log_coeffs, pressure, source, vandermonde, weights):
    plane = (OWN, X, X)
    group = PLANES * OWNERS
    in_hbm = pl.BlockSpec(memory_space=pltpu.HBM)
    packed = call(
        pack_kernel,
        [((group * SENT, X), BF16)],
        [
            ((2, *plane), BF16), ((X, X), F32), ((DOWN + 8, X), F32),
            ((4 * X, 4 * X), BF16), ((OWN * X, X), BF16), ((2 * M + 2 * DOWN, 4 * X), BF16),
            ((ACROSS * DOWN, OWN * X), BF16), ((group * SENT, X), F32), pltpu.SemaphoreType.DMA((2, OWN)),
        ],
        10**6,
        in_specs=[in_hbm] * 2,
    )(*[pltpu.with_memory_space_constraint(field.reshape(plane), pltpu.HBM) for field in (log_coeffs, pressure)])
    got = exchange(packed.reshape(group, SENT // 2, 2, X))
    upper = neighbour(got[0:OWNERS, 4:7], -1).reshape(M, X)
    lower = neighbour(got[group - OWNERS : group], 1).reshape(OWNERS * SENT, X)
    own = call(
        own_kernel,
        [
            ((Q, M), BF16), ((Q, M), BF16), ((M, Q), BF16), ((M, Q), BF16),
            ((Q, CELLS), F32), ((Q, CELLS), F32), ((group, 8, X), F32),
        ],
        [
            ((group * SENT, X), F32), ((M, X), F32), ((M, Q), F32),
            ((M, CELLS), BF16), ((M, CELLS), BF16), ((M, CELLS), BF16), ((M, CELLS), BF16),
            ((PLANES * M, X), BF16), ((2, group, X), BF16), ((group, 12 * X), BF16), ((X, 12 * X), BF16),
        ],
        10**9,
    )(got.reshape(group * SENT, X), vandermonde, weights.reshape(1, Q))
    back = call(
        join_kernel,
        [((group, 8, X), BF16)],
        [((OWNERS * SENT, X), F32), ((M, X), F32), ((M, 3 * X), BF16), ((group, 8, X), F32)],
        10**9,
    )(upper, lower, *own)
    returned = exchange(back)
    result = call(
        finish_kernel,
        [(plane, BF16)],
        [
            ((ACROSS, DOWN, 8, X), F32), ((DOWN + 8, X), F32), ((4 * X, 4 * X), BF16),
            ((X, OWN * X), BF16), ((M + 3 * DOWN, 4 * X), BF16), ((group, X), BF16),
            ((X, X), F32), (plane, BF16), pltpu.SemaphoreType.DMA((OWN,)),
        ],
        10**6,
        out_specs=in_hbm,
    )(returned.reshape(ACROSS, DOWN, 8, X), source.reshape(plane))
    return result.reshape(OWN, 1, X, X)


def solution(mesh):
    grid = Mesh(mesh.devices.reshape(-1, PLANES, OWNERS), ("x", "y", "mode"))
    placed = P("mode", ("x", "y"), None, None)
    return jax.shard_map(
        shards, mesh=grid, in_specs=(placed, placed, placed, P(), P()), out_specs=placed, check_vma=False
    )
```

```python
import jax
import jax.numpy as jnp
from jax import lax
from jax.experimental import pallas as pl
from jax.experimental.pallas import tpu as pltpu
from jax.sharding import Mesh
from jax.sharding import PartitionSpec as P

F32 = jnp.float32
BF16 = jnp.bfloat16
OWN = 6
OWNERS = 32
M = OWN * OWNERS
Q = 512
X = 128
PLANES = 4
ROWS = 4
COLS = 32
ACROSS = 4
DOWN = 32
CELLS = PLANES * X
SENT = 14
VMEM = 48 * 1024 * 1024


def halves(values):
    high = values.astype(BF16)
    return high, (values - high.astype(F32)).astype(BF16)


def dot(a, b):
    return jnp.dot(a, b, preferred_element_type=F32)


def expand(vh_ref, vl_ref, field):
    return dot(vh_ref[...], field) + dot(vl_ref[...], field)


def project(ph_ref, flux):
    fh, fl = halves(flux)
    return dot(ph_ref[...], fh) + dot(ph_ref[...], fl)


def lane_of(rows):
    return lax.broadcasted_iota(jnp.int32, (rows, X), 1)


def turn(values, lanes):
    lanes = lanes % X
    return pltpu.roll(values, lanes, 1) if lanes else values


def grid_of(rows, columns):
    return tuple(lax.broadcasted_iota(jnp.int32, (rows, columns), axis) for axis in (0, 1))


def select(flags):
    return flags.astype(F32).astype(BF16)


def swapper():
    row, col = grid_of(4 * X, 4 * X)
    return select(row == col % X // COLS * X + col // X * COLS + col % COLS)


def start_all(copies):
    for copy in copies:
        copy.start()
    return copies


def fill_tables(past_ref, beside_ref):
    row, col = grid_of(X, X)
    within = col % COLS
    for m in range(4):
        past_ref[:, m * X : (m + 1) * X] = select((col >= 96) & (row == col - 96 + COLS * m))
    for m in range(OWN):
        at = (4 + m) * X
        past_ref[:, at : at + X] = select((within == COLS - 1) & (row == col - 5 + m))
    for m in range(4, OWN):
        at = (6 + m) * X
        half = jnp.where(col >= 112, 80, 96)
        past_ref[:, at : at + X] = select((col >= 96) & (row == col - half + 64 * (m - 4)))
    for m in range(OWN):
        here = select((within == 0) & (row == (col + X - COLS) % X + 26 + m))
        beside_ref[:, m * X : (m + 1) * X] = here


def fill_matrices(turned_ref, weights_ref, vh_ref, vl_ref, ph_ref, chunk, ordered):
    for c in range(Q // X):
        points = slice(c * X, (c + 1) * X)
        chunk[...] = turned_ref[:, points]
        for m in range(OWN):
            ordered[m * OWNERS : (m + 1) * OWNERS, points] = chunk[pl.ds(m, OWNERS, stride=OWN), :]
    vh_ref[...], vl_ref[...] = halves(jnp.transpose(ordered[...]))
    ph_ref[...] = (ordered[...] * weights_ref[...]).astype(BF16)


def pack_kernel(
    log_any, pressure_any, turned_any, weights_any,
    out_ref, vh_ref, vl_ref, ph_ref, past_ref, swap, beside_ref,
    planes, flat, ring, shift, cells, heads, block, turned, weights, chunk, ordered, sems, table_sems,
):
    copies = start_all([
        pltpu.make_async_copy(ref.at[m], planes.at[field, m], sems.at[field, m])
        for field, ref in enumerate((log_any, pressure_any))
        for m in range(OWN)
    ])
    tables = start_all([
        pltpu.make_async_copy(turned_any, turned, table_sems.at[0]),
        pltpu.make_async_copy(weights_any, weights, table_sems.at[1]),
    ])
    swap[...] = swapper()
    fill_tables(past_ref, beside_ref)
    row, col = grid_of(X, X)
    for m in range(OWN):
        shift[m * X : (m + 1) * X, :] = select((col % COLS == 26 + m) & (row == col - 26 - m))
    for field in range(2):
        for m in range(OWN):
            copies[field * OWN + m].wait()
            flat[...] = planes[field, m].astype(F32)
            rows = slice((field * OWN + m) * DOWN, (field * OWN + m + 1) * DOWN)
            for j in range(ROWS):
                cells[rows, j * X : (j + 1) * X] = flat[pl.ds(j, DOWN, stride=ROWS), :].astype(BF16)
            if field:
                ring[0:DOWN, :] = flat[pl.ds(0, DOWN, stride=ROWS), :]
                ring[DOWN : DOWN + 1, :] = flat[0:1, :]
                after = ring[1 : DOWN + 1, :]
                if m < 4:
                    cells[2 * M : 2 * M + DOWN, m * X : (m + 1) * X] = after.astype(BF16)
                else:
                    at = 2 * (m - 4) * X
                    cells[2 * M + DOWN :, at : at + X] = after.astype(BF16)
                    cells[2 * M + DOWN :, at + X : at + 2 * X] = turn(after, -16).astype(BF16)
    swapped = dot(cells[...], swap[...])
    for b in range(ACROSS):
        start = SENT * DOWN * b
        for field, offset in enumerate((0, 8)):
            for m in range(OWN):
                rows = slice((field * OWN + m) * DOWN, (field * OWN + m + 1) * DOWN)
                total = swapped[rows, b * X : (b + 1) * X]
                block[pl.ds(start + offset + m, DOWN, stride=SENT), :] = total
                if field:
                    left = (b - 1) % ACROSS
                    heads[left * DOWN : (left + 1) * DOWN, m * X : (m + 1) * X] = total.astype(BF16)
        block[pl.ds(start + 6, DOWN, stride=SENT), :] = swapped[2 * M : 2 * M + DOWN, b * X : (b + 1) * X]
    rights = dot(heads[...], shift[...])
    within = lane_of(DOWN) % COLS
    for b in range(ACROSS):
        ends = swapped[2 * M + DOWN :, b * X : (b + 1) * X]
        total = jnp.where(within < 16, ends, rights[b * DOWN : (b + 1) * DOWN])
        block[pl.ds(SENT * DOWN * b + 7, DOWN, stride=SENT), :] = total
    out_ref[...] = block[...].astype(BF16)
    for copy in tables:
        copy.wait()
    fill_matrices(turned, weights, vh_ref, vl_ref, ph_ref, chunk, ordered)


def own_kernel(
    got_ref, vh_ref, vl_ref, ph_ref, columns,
    factor_ref, field_ref, block_ref,
    wide, logs, press, right, below, cells, ends, edges,
):
    row, col = grid_of(X, X)
    within = col % COLS
    wide[...] = got_ref[...].astype(F32)
    for k in range(PLANES):
        lanes = slice(k * X, (k + 1) * X)
        for r in range(2):
            ends[r, k * OWNERS : (k + 1) * OWNERS, :] = wide[
                pl.ds(SENT * OWNERS * k + 6 + r, OWNERS, stride=SENT), :
            ].astype(BF16)
        for m in range(OWN):
            modes = slice(m * OWNERS, (m + 1) * OWNERS)
            logs[modes, lanes] = wide[pl.ds(SENT * OWNERS * k + m, OWNERS, stride=SENT), :].astype(BF16)
            here = wide[pl.ds(SENT * OWNERS * k + 8 + m, OWNERS, stride=SENT), :].astype(BF16)
            press[modes, lanes] = here
            cells[m, k * OWNERS : (k + 1) * OWNERS, :] = here
    next_x = select((within < COLS - 1) & (row == col + 1))
    next_y = select(row == col + COLS)
    for m in range(OWN):
        modes = slice(m * OWNERS, (m + 1) * OWNERS)
        at = (4 + m) * X
        to_right = dot(cells[m], next_x) + dot(ends[1], columns[:, at : at + X])
        at = (m if m < 4 else 6 + m) * X
        to_below = dot(cells[m], next_y) + dot(ends[m // 4], columns[:, at : at + X])
        for k in range(PLANES):
            lanes = slice(k * X, (k + 1) * X)
            owners = slice(k * OWNERS, (k + 1) * OWNERS)
            right[modes, lanes] = to_right[owners].astype(BF16)
            below[modes, lanes] = to_below[owners].astype(BF16)
    factor_ref[...] = jnp.exp(expand(vh_ref, vl_ref, logs[...]))
    field_ref[...] = dot(vh_ref[...], press[...])
    flux_x = factor_ref[...] * (dot(vh_ref[...], right[...]) - field_ref[...])
    proj_x = project(ph_ref, flux_x)
    flux_y = factor_ref[...] * (dot(vh_ref[...], below[...]) - field_ref[...])
    proj_y = project(ph_ref, flux_y)
    inner = CELLS - X
    flux_z = factor_ref[:, 0:inner] * (field_ref[:, X:CELLS] - field_ref[:, 0:inner])
    proj_z = project(ph_ref, flux_z)
    xh, xl = halves(proj_x)
    yh, yl = halves(proj_y)
    less_x = (row == col).astype(F32) - ((within > 0) & (row == col - 1)).astype(F32)
    less_x = less_x.astype(BF16)
    less_y = ((row == col).astype(F32) - (row == col - COLS).astype(F32)).astype(BF16)
    for k in range(PLANES):
        lanes = slice(k * X, (k + 1) * X)
        owners = slice(k * OWNERS, (k + 1) * OWNERS)
        total = dot(xh[:, lanes], less_x) + dot(xl[:, lanes], less_x)
        total = total + dot(yh[:, lanes], less_y) + dot(yl[:, lanes], less_y)
        if k < PLANES - 1:
            total = total + proj_z[:, lanes]
        if k > 0:
            total = total - proj_z[:, (k - 1) * X : k * X]
        for m in range(OWN):
            modes = slice(m * OWNERS, (m + 1) * OWNERS)
            block_ref[owners, m, :] = total[modes]
            at = (m if m < 4 else 6 + m) * X
            edges[owners, at : at + X] = yh[modes, lanes]
            edges[owners, (4 + m) * X : (5 + m) * X] = xh[modes, lanes]
    back = (((1,), (1,)), ((), ()))
    block_ref[:, 6, :] = lax.dot_general(
        edges[:, 0 : 4 * X], columns[:, 0 : 4 * X], back, preferred_element_type=F32
    )
    block_ref[:, 7, :] = lax.dot_general(
        edges[:, 4 * X :], columns[:, 4 * X :], back, preferred_element_type=F32
    )


def join_kernel(
    upper_ref, lower_ref, vh_ref, vl_ref, ph_ref, factor_ref, field_ref, block_ref,
    out_ref,
    wide, above, faces, block,
):
    above[...] = upper_ref[...].astype(F32)
    wide[...] = lower_ref[...].astype(F32)
    for m in range(OWN):
        modes = slice(m * OWNERS, (m + 1) * OWNERS)
        faces[modes, 0:X] = above[pl.ds(m, OWNERS, stride=OWN), :].astype(BF16)
        faces[modes, X : 2 * X] = wide[pl.ds(m, OWNERS, stride=SENT), :].astype(BF16)
        faces[modes, 2 * X : 3 * X] = wide[pl.ds(8 + m, OWNERS, stride=SENT), :].astype(BF16)
    last = slice(CELLS - X, CELLS)
    values = dot(vh_ref[...], faces[...])
    top = factor_ref[:, last] * (values[:, 0:X] - field_ref[:, last])
    logs = values[:, X : 2 * X] + dot(vl_ref[...], faces[:, X : 2 * X])
    bottom = jnp.exp(logs) * (field_ref[:, 0:X] - values[:, 2 * X : 3 * X])
    both = project(ph_ref, jnp.concatenate([bottom, top], axis=1))
    block[...] = block_ref[...]
    for m in range(OWN):
        modes = slice(m * OWNERS, (m + 1) * OWNERS)
        block[0:OWNERS, m, :] -= both[modes, 0:X]
        block[3 * OWNERS : 4 * OWNERS, m, :] += both[modes, X : 2 * X]
    out_ref[...] = block[...].astype(BF16)


def finish_kernel(got_ref, source_ref, swap, shift, out_any, wide, ring, cells, ends, flat, planes, sems):
    wide[...] = got_ref[...].astype(F32)
    for b in range(ACROSS):
        lanes = slice(b * X, (b + 1) * X)
        for m in range(OWN):
            cells[m * DOWN : (m + 1) * DOWN, lanes] = wide[b, :, m, :].astype(BF16)
        cells[M : M + DOWN, lanes] = wide[b, :, 7, :].astype(BF16)
        for r in range(2):
            ring[1 : DOWN + 1, :] = wide[b, :, 6 + r, :]
            ring[0:1, :] = wide[b, DOWN - 1 : DOWN, 6 + r, :]
            at = M + (1 + r) * DOWN
            cells[at : at + DOWN, lanes] = ring[0:DOWN, :].astype(BF16)
    swapped = dot(cells[...], swap[...])
    for j in range(ROWS):
        ends[j * DOWN : (j + 1) * DOWN, :] = swapped[M : M + DOWN, j * X : (j + 1) * X].astype(BF16)
    beside = dot(ends[...], shift[...])
    above = swapped[M + DOWN : M + 2 * DOWN]
    halved = swapped[M + 2 * DOWN :]
    inside = lane_of(DOWN) % COLS < 16
    copies = []
    for m in range(OWN):
        modes = slice(m * DOWN, (m + 1) * DOWN)
        for j in range(ROWS):
            total = swapped[modes, j * X : (j + 1) * X]
            total = total - beside[j * DOWN : (j + 1) * DOWN, m * X : (m + 1) * X]
            if j == 0 and m < 4:
                total = total - above[:, m * X : (m + 1) * X]
            elif j == 0:
                at = 2 * (m - 4) * X
                far = turn(halved[:, at + X : at + 2 * X], 16)
                total = total - jnp.where(inside, halved[:, at : at + X], far)
            flat[pl.ds(j, DOWN, stride=ROWS), :] = total
        planes[m] = (-flat[...] - source_ref[m].astype(F32)).astype(BF16)
        copies.append(pltpu.make_async_copy(planes.at[m], out_any.at[m], sems.at[m]))
        copies[m].start()
    for copy in copies:
        copy.wait()


def call(kernel, outs, scratch, cost, **rest):
    outs = [jax.ShapeDtypeStruct(shape, dtype) for shape, dtype in outs]
    scratch = [pltpu.VMEM(*entry) if isinstance(entry, tuple) else entry for entry in scratch]
    return pl.pallas_call(
        kernel,
        out_shape=outs if len(outs) > 1 else outs[0],
        scratch_shapes=scratch,
        compiler_params=pltpu.CompilerParams(vmem_limit_bytes=VMEM),
        cost_estimate=pl.CostEstimate(flops=cost, bytes_accessed=2**20, transcendentals=0),
        **rest,
    )


def neighbour(block, distance):
    devices = range(lax.axis_size("x"))
    route = [((i - distance) % len(devices), i) for i in devices]
    return lax.ppermute(block, "x", route)


def exchange(block):
    return lax.all_to_all(block, ("y", "mode"), split_axis=0, concat_axis=0, tiled=True)


def shards(log_coeffs, pressure, source, vandermonde, weights):
    plane = (OWN, X, X)
    group = PLANES * OWNERS
    in_hbm = pl.BlockSpec(memory_space=pltpu.HBM)
    packed, vh, vl, ph, past, swap, beside = call(
        pack_kernel,
        [
            ((group * SENT, X), BF16), ((Q, M), BF16), ((Q, M), BF16), ((M, Q), BF16),
            ((X, 12 * X), BF16), ((4 * X, 4 * X), BF16), ((X, OWN * X), BF16),
        ],
        [
            ((2, *plane), BF16), ((X, X), F32), ((DOWN + 8, X), F32),
            ((OWN * X, X), BF16), ((2 * M + 2 * DOWN, 4 * X), BF16),
            ((ACROSS * DOWN, OWN * X), BF16), ((group * SENT, X), F32),
            ((M, Q), F32), ((1, Q), F32), ((M, X), F32), ((M, Q), F32),
            pltpu.SemaphoreType.DMA((2, OWN)), pltpu.SemaphoreType.DMA((2,)),
        ],
        10**6,
        in_specs=[in_hbm] * 4,
    )(*[
        pltpu.with_memory_space_constraint(array, pltpu.HBM)
        for array in (
            log_coeffs.reshape(plane), pressure.reshape(plane), vandermonde.T, weights.reshape(1, Q)
        )
    ])
    halved = (vh, vl, ph)
    got = exchange(packed.reshape(group, SENT // 2, 2, X))
    upper = neighbour(got[0:OWNERS, 4:7], -1).reshape(M, X)
    lower = neighbour(got[group - OWNERS : group], 1).reshape(OWNERS * SENT, X)
    own = call(
        own_kernel,
        [((Q, CELLS), F32), ((Q, CELLS), F32), ((group, 8, X), F32)],
        [
            ((group * SENT, X), F32),
            ((M, CELLS), BF16), ((M, CELLS), BF16), ((M, CELLS), BF16), ((M, CELLS), BF16),
            ((OWN, group, X), BF16), ((2, group, X), BF16), ((group, 12 * X), BF16),
        ],
        10**9,
    )(got.reshape(group * SENT, X), *halved, past)
    back = call(
        join_kernel,
        [((group, 8, X), BF16)],
        [((OWNERS * SENT, X), F32), ((M, X), F32), ((M, 3 * X), BF16), ((group, 8, X), F32)],
        10**9,
    )(upper, lower, *halved, *own)
    returned = exchange(back)
    result = call(
        finish_kernel,
        [(plane, BF16)],
        [
            ((ACROSS, DOWN, 8, X), F32), ((DOWN + 8, X), F32), ((M + 3 * DOWN, 4 * X), BF16),
            ((group, X), BF16), ((X, X), F32), (plane, BF16), pltpu.SemaphoreType.DMA((OWN,)),
        ],
        10**6,
        out_specs=in_hbm,
    )(returned.reshape(ACROSS, DOWN, 8, X), source.reshape(plane), swap, beside)
    return result.reshape(OWN, 1, X, X)


def solution(mesh):
    grid = Mesh(mesh.devices.reshape(-1, PLANES, OWNERS), ("x", "y", "mode"))
    placed = P("mode", ("x", "y"), None, None)
    return jax.shard_map(
        shards, mesh=grid, in_specs=(placed, placed, placed, P(), P()), out_specs=placed, check_vma=False
    )
```

```python
import jax
import jax.numpy as jnp
from jax import lax
from jax.experimental import pallas as pl
from jax.experimental.pallas import tpu as pltpu
from jax.sharding import Mesh
from jax.sharding import PartitionSpec as P

F32 = jnp.float32
BF16 = jnp.bfloat16
OWN = 6
OWNERS = 32
M = OWN * OWNERS
Q = 512
X = 128
PLANES = 4
ROWS = 4
COLS = 32
ACROSS = 4
DOWN = 32
CELLS = PLANES * X
SENT = 14
VMEM = 48 * 1024 * 1024


def halves(values):
    high = values.astype(BF16)
    return high, (values - high.astype(F32)).astype(BF16)


def dot(a, b):
    return jnp.dot(a, b, preferred_element_type=F32)


def expand(vh_ref, vl_ref, field):
    return dot(vh_ref[...], field) + dot(vl_ref[...], field)


def project(ph_ref, flux):
    fh, fl = halves(flux)
    return dot(ph_ref[...], fh) + dot(ph_ref[...], fl)


def lane_of(rows):
    return lax.broadcasted_iota(jnp.int32, (rows, X), 1)


def turn(values, lanes):
    lanes = lanes % X
    return pltpu.roll(values, lanes, 1) if lanes else values


def grid_of(rows, columns):
    return tuple(lax.broadcasted_iota(jnp.int32, (rows, columns), axis) for axis in (0, 1))


def select(flags):
    return flags.astype(F32).astype(BF16)


def swapper():
    row, col = grid_of(4 * X, 4 * X)
    return select(row == col % X // COLS * X + col // X * COLS + col % COLS)


def start_all(copies):
    for copy in copies:
        copy.start()
    return copies


def fill_tables(past_ref, beside_ref):
    row, col = grid_of(X, X)
    within = col % COLS
    for m in range(4):
        past_ref[:, m * X : (m + 1) * X] = select((col >= 96) & (row == col - 96 + COLS * m))
    for m in range(OWN):
        at = (4 + m) * X
        past_ref[:, at : at + X] = select((within == COLS - 1) & (row == col - 5 + m))
    for m in range(4, OWN):
        at = (6 + m) * X
        half = jnp.where(col >= 112, 80, 96)
        past_ref[:, at : at + X] = select((col >= 96) & (row == col - half + 64 * (m - 4)))
    for m in range(OWN):
        here = select((within == 0) & (row == (col + X - COLS) % X + 26 + m))
        beside_ref[:, m * X : (m + 1) * X] = here


def fill_matrices(turned_ref, weights_ref, vh_ref, vl_ref, ph_ref, chunk, ordered):
    for c in range(Q // X):
        points = slice(c * X, (c + 1) * X)
        chunk[0:M] = turned_ref[:, points]
        for m in range(OWN):
            ordered[m * OWNERS : (m + 1) * OWNERS, points] = chunk[pl.ds(m, OWNERS, stride=OWN), :]
    vh_ref[...], vl_ref[...] = halves(jnp.transpose(ordered[...]))
    ph_ref[...] = (ordered[...] * weights_ref[...]).astype(BF16)


def pack_kernel(
    log_any, pressure_any, turned_any, weights_any,
    out_ref, vh_ref, vl_ref, ph_ref, past_ref, swap, beside_ref,
    planes, flat, ring, shift, cells, heads, block, turned, weights, chunk, ordered, sems, table_sems,
):
    copies = start_all([
        pltpu.make_async_copy(ref.at[m], planes.at[field, m], sems.at[field, m])
        for field, ref in enumerate((log_any, pressure_any))
        for m in range(OWN)
    ])
    tables = start_all([
        pltpu.make_async_copy(turned_any, turned, table_sems.at[0]),
        pltpu.make_async_copy(weights_any, weights, table_sems.at[1]),
    ])
    swap[...] = swapper()
    fill_tables(past_ref, beside_ref)
    row, col = grid_of(X, X)
    for m in range(OWN):
        shift[m * X : (m + 1) * X, :] = select((col % COLS == 26 + m) & (row == col - 26 - m))
    for field in range(2):
        for m in range(OWN):
            copies[field * OWN + m].wait()
            flat[0:X] = planes[field, m].astype(F32)
            rows = slice((field * OWN + m) * DOWN, (field * OWN + m + 1) * DOWN)
            for j in range(ROWS):
                cells[rows, j * X : (j + 1) * X] = flat[pl.ds(j, DOWN, stride=ROWS), :].astype(BF16)
            if field:
                ring[0:DOWN, :] = flat[pl.ds(0, DOWN, stride=ROWS), :]
                ring[DOWN : DOWN + 1, :] = flat[0:1, :]
                after = ring[1 : DOWN + 1, :]
                if m < 4:
                    cells[2 * M : 2 * M + DOWN, m * X : (m + 1) * X] = after.astype(BF16)
                else:
                    at = 2 * (m - 4) * X
                    cells[2 * M + DOWN :, at : at + X] = after.astype(BF16)
                    cells[2 * M + DOWN :, at + X : at + 2 * X] = turn(after, -16).astype(BF16)
    swapped = dot(cells[...], swap[...])
    for b in range(ACROSS):
        start = SENT * DOWN * b
        for field, offset in enumerate((0, OWN)):
            for m in range(OWN):
                rows = slice((field * OWN + m) * DOWN, (field * OWN + m + 1) * DOWN)
                total = swapped[rows, b * X : (b + 1) * X]
                block[pl.ds(start + offset + m, DOWN, stride=SENT), :] = total
                if field:
                    left = (b - 1) % ACROSS
                    heads[left * DOWN : (left + 1) * DOWN, m * X : (m + 1) * X] = total.astype(BF16)
        block[pl.ds(start + 12, DOWN, stride=SENT), :] = swapped[2 * M : 2 * M + DOWN, b * X : (b + 1) * X]
    rights = dot(heads[...], shift[...])
    within = lane_of(DOWN) % COLS
    for b in range(ACROSS):
        ends = swapped[2 * M + DOWN :, b * X : (b + 1) * X]
        total = jnp.where(within < 16, ends, rights[b * DOWN : (b + 1) * DOWN])
        block[pl.ds(SENT * DOWN * b + 13, DOWN, stride=SENT), :] = total
    out_ref[...] = block[0 : out_ref.shape[0]].astype(BF16)
    for copy in tables:
        copy.wait()
    fill_matrices(turned, weights, vh_ref, vl_ref, ph_ref, chunk, ordered)


def own_kernel(
    got_ref, vh_ref, vl_ref, ph_ref, columns,
    factor_ref, field_ref, block_ref,
    wide, logs, press, right, below, cells, ends, edges,
):
    row, col = grid_of(X, X)
    within = col % COLS
    wide[0 : got_ref.shape[0]] = got_ref[...].astype(F32)
    for k in range(PLANES):
        lanes = slice(k * X, (k + 1) * X)
        for r in range(2):
            ends[r, k * OWNERS : (k + 1) * OWNERS, :] = wide[
                pl.ds(SENT * OWNERS * k + 12 + r, OWNERS, stride=SENT), :
            ].astype(BF16)
        for m in range(OWN):
            modes = slice(m * OWNERS, (m + 1) * OWNERS)
            logs[modes, lanes] = wide[pl.ds(SENT * OWNERS * k + m, OWNERS, stride=SENT), :].astype(BF16)
            here = wide[pl.ds(SENT * OWNERS * k + 6 + m, OWNERS, stride=SENT), :].astype(BF16)
            press[modes, lanes] = here
            cells[m, k * OWNERS : (k + 1) * OWNERS, :] = here
    next_x = select((within < COLS - 1) & (row == col + 1))
    next_y = select(row == col + COLS)
    for m in range(OWN):
        modes = slice(m * OWNERS, (m + 1) * OWNERS)
        at = (4 + m) * X
        to_right = dot(cells[m], next_x) + dot(ends[1], columns[:, at : at + X])
        at = (m if m < 4 else 6 + m) * X
        to_below = dot(cells[m], next_y) + dot(ends[m // 4], columns[:, at : at + X])
        for k in range(PLANES):
            lanes = slice(k * X, (k + 1) * X)
            owners = slice(k * OWNERS, (k + 1) * OWNERS)
            right[modes, lanes] = to_right[owners].astype(BF16)
            below[modes, lanes] = to_below[owners].astype(BF16)
    factor_ref[...] = jnp.exp(expand(vh_ref, vl_ref, logs[...]))
    field_ref[...] = dot(vh_ref[...], press[...])
    flux_x = factor_ref[...] * (dot(vh_ref[...], right[...]) - field_ref[...])
    proj_x = project(ph_ref, flux_x)
    flux_y = factor_ref[...] * (dot(vh_ref[...], below[...]) - field_ref[...])
    proj_y = project(ph_ref, flux_y)
    inner = CELLS - X
    flux_z = factor_ref[:, 0:inner] * (field_ref[:, X:CELLS] - field_ref[:, 0:inner])
    proj_z = project(ph_ref, flux_z)
    xh, xl = halves(proj_x)
    yh, yl = halves(proj_y)
    less_x = (row == col).astype(F32) - ((within > 0) & (row == col - 1)).astype(F32)
    less_x = less_x.astype(BF16)
    less_y = ((row == col).astype(F32) - (row == col - COLS).astype(F32)).astype(BF16)
    for k in range(PLANES):
        lanes = slice(k * X, (k + 1) * X)
        owners = slice(k * OWNERS, (k + 1) * OWNERS)
        total = dot(xh[:, lanes], less_x) + dot(xl[:, lanes], less_x)
        total = total + dot(yh[:, lanes], less_y) + dot(yl[:, lanes], less_y)
        if k < PLANES - 1:
            total = total + proj_z[:, lanes]
        if k > 0:
            total = total - proj_z[:, (k - 1) * X : k * X]
        for m in range(OWN):
            modes = slice(m * OWNERS, (m + 1) * OWNERS)
            block_ref[owners, m, :] = total[modes]
            at = (m if m < 4 else 6 + m) * X
            edges[owners, at : at + X] = yh[modes, lanes]
            edges[owners, (4 + m) * X : (5 + m) * X] = xh[modes, lanes]
    back = (((1,), (1,)), ((), ()))
    block_ref[:, 6, :] = lax.dot_general(
        edges[:, 0 : 4 * X], columns[:, 0 : 4 * X], back, preferred_element_type=F32
    )
    block_ref[:, 7, :] = lax.dot_general(
        edges[:, 4 * X :], columns[:, 4 * X :], back, preferred_element_type=F32
    )


def join_kernel(
    upper_ref, lower_ref, vh_ref, vl_ref, ph_ref, factor_ref, field_ref, block_ref,
    out_ref,
    wide, above, faces, block,
):
    above[0:M] = upper_ref[...].astype(F32)
    wide[0 : 2 * M] = lower_ref[...].astype(F32)
    for m in range(OWN):
        modes = slice(m * OWNERS, (m + 1) * OWNERS)
        faces[modes, 0:X] = above[pl.ds(m, OWNERS, stride=OWN), :].astype(BF16)
        faces[modes, X : 2 * X] = wide[pl.ds(m, OWNERS, stride=2 * OWN), :].astype(BF16)
        faces[modes, 2 * X : 3 * X] = wide[pl.ds(OWN + m, OWNERS, stride=2 * OWN), :].astype(BF16)
    last = slice(CELLS - X, CELLS)
    values = dot(vh_ref[...], faces[...])
    top = factor_ref[:, last] * (values[:, 0:X] - field_ref[:, last])
    logs = values[:, X : 2 * X] + dot(vl_ref[...], faces[:, X : 2 * X])
    bottom = jnp.exp(logs) * (field_ref[:, 0:X] - values[:, 2 * X : 3 * X])
    both = project(ph_ref, jnp.concatenate([bottom, top], axis=1))
    block[...] = block_ref[...]
    for m in range(OWN):
        modes = slice(m * OWNERS, (m + 1) * OWNERS)
        block[0:OWNERS, m, :] -= both[modes, 0:X]
        block[3 * OWNERS : 4 * OWNERS, m, :] += both[modes, X : 2 * X]
    out_ref[...] = block[...].astype(BF16)


def finish_kernel(got_ref, source_ref, swap, shift, out_any, wide, ring, cells, ends, flat, planes, sems):
    wide[...] = got_ref[...].astype(F32)
    for b in range(ACROSS):
        lanes = slice(b * X, (b + 1) * X)
        for m in range(OWN):
            cells[m * DOWN : (m + 1) * DOWN, lanes] = wide[b, :, m, :].astype(BF16)
        cells[M : M + DOWN, lanes] = wide[b, :, 7, :].astype(BF16)
        for r in range(2):
            ring[1 : DOWN + 1, :] = wide[b, :, 6 + r, :]
            ring[0:1, :] = wide[b, DOWN - 1 : DOWN, 6 + r, :]
            at = M + (1 + r) * DOWN
            cells[at : at + DOWN, lanes] = ring[0:DOWN, :].astype(BF16)
    swapped = dot(cells[...], swap[...])
    for j in range(ROWS):
        ends[j * DOWN : (j + 1) * DOWN, :] = swapped[M : M + DOWN, j * X : (j + 1) * X].astype(BF16)
    beside = dot(ends[...], shift[...])
    above = swapped[M + DOWN : M + 2 * DOWN]
    halved = swapped[M + 2 * DOWN :]
    inside = lane_of(DOWN) % COLS < 16
    copies = []
    for m in range(OWN):
        modes = slice(m * DOWN, (m + 1) * DOWN)
        for j in range(ROWS):
            total = swapped[modes, j * X : (j + 1) * X]
            total = total - beside[j * DOWN : (j + 1) * DOWN, m * X : (m + 1) * X]
            if j == 0 and m < 4:
                total = total - above[:, m * X : (m + 1) * X]
            elif j == 0:
                at = 2 * (m - 4) * X
                far = turn(halved[:, at + X : at + 2 * X], 16)
                total = total - jnp.where(inside, halved[:, at : at + X], far)
            flat[pl.ds(j, DOWN, stride=ROWS), :] = total
        planes[m] = (-flat[0:X] - source_ref[m].astype(F32)).astype(BF16)
        copies.append(pltpu.make_async_copy(planes.at[m], out_any.at[m], sems.at[m]))
        copies[m].start()
    for copy in copies:
        copy.wait()


def call(kernel, outs, scratch, cost, **rest):
    outs = [jax.ShapeDtypeStruct(shape, dtype) for shape, dtype in outs]
    scratch = [pltpu.VMEM(*entry) if isinstance(entry, tuple) else entry for entry in scratch]
    return pl.pallas_call(
        kernel,
        out_shape=outs if len(outs) > 1 else outs[0],
        scratch_shapes=scratch,
        compiler_params=pltpu.CompilerParams(vmem_limit_bytes=VMEM),
        cost_estimate=pl.CostEstimate(flops=cost, bytes_accessed=2**20, transcendentals=0),
        **rest,
    )


def neighbour(block, distance):
    devices = range(lax.axis_size("x"))
    route = [((i - distance) % len(devices), i) for i in devices]
    return lax.ppermute(block, "x", route)


def exchange(block):
    return lax.all_to_all(block, ("y", "mode"), split_axis=0, concat_axis=0, tiled=True)


def shards(log_coeffs, pressure, source, vandermonde, weights):
    plane = (OWN, X, X)
    group = PLANES * OWNERS
    in_hbm = pl.BlockSpec(memory_space=pltpu.HBM)
    packed, vh, vl, ph, past, swap, beside = call(
        pack_kernel,
        [
            ((group * SENT, X), BF16), ((Q, M), BF16), ((Q, M), BF16), ((M, Q), BF16),
            ((X, 12 * X), BF16), ((4 * X, 4 * X), BF16), ((X, OWN * X), BF16),
        ],
        [
            ((2, *plane), BF16), ((X + 8, X), F32), ((DOWN + 8, X), F32),
            ((OWN * X, X), BF16), ((2 * M + 2 * DOWN, 4 * X), BF16),
            ((ACROSS * DOWN, OWN * X), BF16), ((group * SENT + 16, X), F32),
            ((M, Q), F32), ((1, Q), F32), ((M + 8, X), F32), ((M, Q), F32),
            pltpu.SemaphoreType.DMA((2, OWN)), pltpu.SemaphoreType.DMA((2,)),
        ],
        10**6,
        in_specs=[in_hbm] * 4,
    )(*[
        pltpu.with_memory_space_constraint(array, pltpu.HBM)
        for array in (
            log_coeffs.reshape(plane), pressure.reshape(plane), vandermonde.T, weights.reshape(1, Q)
        )
    ])
    halved = (vh, vl, ph)
    got = exchange(packed.reshape(group, SENT // 2, 2, X))
    upper = neighbour(got[0:OWNERS, 3:6], -1).reshape(M, X)
    lower = neighbour(got[group - OWNERS : group, 0:6], 1).reshape(2 * M, X)
    own = call(
        own_kernel,
        [((Q, CELLS), F32), ((Q, CELLS), F32), ((group, 8, X), F32)],
        [
            ((group * SENT + 16, X), F32),
            ((M, CELLS), BF16), ((M, CELLS), BF16), ((M, CELLS), BF16), ((M, CELLS), BF16),
            ((OWN, group, X), BF16), ((2, group, X), BF16), ((group, 12 * X), BF16),
        ],
        10**9,
    )(got.reshape(group * SENT, X), *halved, past)
    back = call(
        join_kernel,
        [((group, 8, X), BF16)],
        [((2 * M + 16, X), F32), ((M + 8, X), F32), ((M, 3 * X), BF16), ((group, 8, X), F32)],
        10**9,
    )(upper, lower, *halved, *own)
    returned = exchange(back)
    result = call(
        finish_kernel,
        [(plane, BF16)],
        [
            ((ACROSS, DOWN, 8, X), F32), ((DOWN + 8, X), F32), ((M + 3 * DOWN, 4 * X), BF16),
            ((group, X), BF16), ((X + 8, X), F32), (plane, BF16), pltpu.SemaphoreType.DMA((OWN,)),
        ],
        10**6,
        out_specs=in_hbm,
    )(returned.reshape(ACROSS, DOWN, 8, X), source.reshape(plane), swap, beside)
    return result.reshape(OWN, 1, X, X)


def solution(mesh):
    grid = Mesh(mesh.devices.reshape(-1, PLANES, OWNERS), ("x", "y", "mode"))
    placed = P("mode", ("x", "y"), None, None)
    return jax.shard_map(
        shards, mesh=grid, in_specs=(placed, placed, placed, P(), P()), out_specs=placed, check_vma=False
    )
```

```python
import jax
import jax.numpy as jnp
from jax import lax
from jax.experimental import pallas as pl
from jax.experimental.pallas import tpu as pltpu
from jax.sharding import Mesh
from jax.sharding import PartitionSpec as P

F32 = jnp.float32
BF16 = jnp.bfloat16
OWN = 6
OWNERS = 32
M = OWN * OWNERS
Q = 512
X = 128
PLANES = 4
ROWS = 4
COLS = 32
ACROSS = 4
DOWN = 32
CELLS = PLANES * X
SENT = 14
VMEM = 48 * 1024 * 1024


def halves(values):
    high = values.astype(BF16)
    return high, (values - high.astype(F32)).astype(BF16)


def dot(a, b):
    return jnp.dot(a, b, preferred_element_type=F32)


def expand(vh_ref, vl_ref, field):
    return dot(vh_ref[...], field) + dot(vl_ref[...], field)


def project(ph_ref, flux):
    fh, fl = halves(flux)
    return dot(ph_ref[...], fh) + dot(ph_ref[...], fl)


def lane_of(rows):
    return lax.broadcasted_iota(jnp.int32, (rows, X), 1)


def turn(values, lanes):
    lanes = lanes % X
    return pltpu.roll(values, lanes, 1) if lanes else values


def grid_of(rows, columns):
    return tuple(lax.broadcasted_iota(jnp.int32, (rows, columns), axis) for axis in (0, 1))


def select(flags):
    return flags.astype(F32).astype(BF16)


def swapper():
    row, col = grid_of(4 * X, 4 * X)
    return select(row == col % X // COLS * X + col // X * COLS + col % COLS)


def start_all(copies):
    for copy in copies:
        copy.start()
    return copies


def fill_tables(past_ref, beside_ref):
    row, col = grid_of(X, X)
    within = col % COLS
    for m in range(4):
        past_ref[:, m * X : (m + 1) * X] = select((col >= 96) & (row == col - 96 + COLS * m))
    for m in range(OWN):
        at = (4 + m) * X
        past_ref[:, at : at + X] = select((within == COLS - 1) & (row == col - 5 + m))
    for m in range(4, OWN):
        at = (6 + m) * X
        half = jnp.where(col >= 112, 80, 96)
        past_ref[:, at : at + X] = select((col >= 96) & (row == col - half + 64 * (m - 4)))
    for m in range(OWN):
        here = select((within == 0) & (row == (col + X - COLS) % X + 26 + m))
        beside_ref[:, m * X : (m + 1) * X] = here


def fill_matrices(turned_ref, weights_ref, vh_ref, vl_ref, ph_ref, chunk, ordered):
    for c in range(Q // X):
        points = slice(c * X, (c + 1) * X)
        chunk[0:M] = turned_ref[:, points]
        for m in range(OWN):
            ordered[m * OWNERS : (m + 1) * OWNERS, points] = chunk[pl.ds(m, OWNERS, stride=OWN), :]
    vh_ref[...], vl_ref[...] = halves(jnp.transpose(ordered[...]))
    ph_ref[...] = (ordered[...] * weights_ref[...]).astype(BF16)


def pack_kernel(
    log_any, pressure_any, weights_any,
    out_ref, weights_ref, past_ref, swap, beside_ref,
    planes, flat, ring, shift, cells, heads, block, sems, weights_sem,
):
    copies = start_all([
        pltpu.make_async_copy(ref.at[m], planes.at[field, m], sems.at[field, m])
        for field, ref in enumerate((log_any, pressure_any))
        for m in range(OWN)
    ])
    moved = pltpu.make_async_copy(weights_any, weights_ref, weights_sem)
    moved.start()
    swap[...] = swapper()
    fill_tables(past_ref, beside_ref)
    row, col = grid_of(X, X)
    for m in range(OWN):
        shift[m * X : (m + 1) * X, :] = select((col % COLS == 26 + m) & (row == col - 26 - m))
    for field in range(2):
        for m in range(OWN):
            copies[field * OWN + m].wait()
            flat[0:X] = planes[field, m].astype(F32)
            rows = slice((field * OWN + m) * DOWN, (field * OWN + m + 1) * DOWN)
            for j in range(ROWS):
                cells[rows, j * X : (j + 1) * X] = flat[pl.ds(j, DOWN, stride=ROWS), :].astype(BF16)
            if field:
                ring[0:DOWN, :] = flat[pl.ds(0, DOWN, stride=ROWS), :]
                ring[DOWN : DOWN + 1, :] = flat[0:1, :]
                after = ring[1 : DOWN + 1, :]
                if m < 4:
                    cells[2 * M : 2 * M + DOWN, m * X : (m + 1) * X] = after.astype(BF16)
                else:
                    at = 2 * (m - 4) * X
                    cells[2 * M + DOWN :, at : at + X] = after.astype(BF16)
                    cells[2 * M + DOWN :, at + X : at + 2 * X] = turn(after, -16).astype(BF16)
    swapped = dot(cells[...], swap[...])
    for b in range(ACROSS):
        start = SENT * DOWN * b
        for field, offset in enumerate((0, OWN)):
            for m in range(OWN):
                rows = slice((field * OWN + m) * DOWN, (field * OWN + m + 1) * DOWN)
                total = swapped[rows, b * X : (b + 1) * X]
                block[pl.ds(start + offset + m, DOWN, stride=SENT), :] = total
                if field:
                    left = (b - 1) % ACROSS
                    heads[left * DOWN : (left + 1) * DOWN, m * X : (m + 1) * X] = total.astype(BF16)
        block[pl.ds(start + 12, DOWN, stride=SENT), :] = swapped[2 * M : 2 * M + DOWN, b * X : (b + 1) * X]
    rights = dot(heads[...], shift[...])
    within = lane_of(DOWN) % COLS
    for b in range(ACROSS):
        ends = swapped[2 * M + DOWN :, b * X : (b + 1) * X]
        total = jnp.where(within < 16, ends, rights[b * DOWN : (b + 1) * DOWN])
        block[pl.ds(SENT * DOWN * b + 13, DOWN, stride=SENT), :] = total
    out_ref[...] = block[0 : out_ref.shape[0]].astype(BF16)
    moved.wait()


def own_kernel(
    got_ref, turned_ref, weights_ref, columns,
    vh_ref, vl_ref, ph_ref, factor_ref, field_ref, block_ref,
    wide, logs, press, right, below, cells, ends, edges, chunk, ordered,
):
    fill_matrices(turned_ref, weights_ref, vh_ref, vl_ref, ph_ref, chunk, ordered)
    row, col = grid_of(X, X)
    within = col % COLS
    wide[0 : got_ref.shape[0]] = got_ref[...].astype(F32)
    for k in range(PLANES):
        lanes = slice(k * X, (k + 1) * X)
        for r in range(2):
            ends[r, k * OWNERS : (k + 1) * OWNERS, :] = wide[
                pl.ds(SENT * OWNERS * k + 12 + r, OWNERS, stride=SENT), :
            ].astype(BF16)
        for m in range(OWN):
            modes = slice(m * OWNERS, (m + 1) * OWNERS)
            logs[modes, lanes] = wide[pl.ds(SENT * OWNERS * k + m, OWNERS, stride=SENT), :].astype(BF16)
            here = wide[pl.ds(SENT * OWNERS * k + 6 + m, OWNERS, stride=SENT), :].astype(BF16)
            press[modes, lanes] = here
            cells[m, k * OWNERS : (k + 1) * OWNERS, :] = here
    next_x = select((within < COLS - 1) & (row == col + 1))
    next_y = select(row == col + COLS)
    for m in range(OWN):
        modes = slice(m * OWNERS, (m + 1) * OWNERS)
        at = (4 + m) * X
        to_right = dot(cells[m], next_x) + dot(ends[1], columns[:, at : at + X])
        at = (m if m < 4 else 6 + m) * X
        to_below = dot(cells[m], next_y) + dot(ends[m // 4], columns[:, at : at + X])
        for k in range(PLANES):
            lanes = slice(k * X, (k + 1) * X)
            owners = slice(k * OWNERS, (k + 1) * OWNERS)
            right[modes, lanes] = to_right[owners].astype(BF16)
            below[modes, lanes] = to_below[owners].astype(BF16)
    factor_ref[...] = jnp.exp(expand(vh_ref, vl_ref, logs[...]))
    field_ref[...] = dot(vh_ref[...], press[...])
    flux_x = factor_ref[...] * (dot(vh_ref[...], right[...]) - field_ref[...])
    proj_x = project(ph_ref, flux_x)
    flux_y = factor_ref[...] * (dot(vh_ref[...], below[...]) - field_ref[...])
    proj_y = project(ph_ref, flux_y)
    inner = CELLS - X
    flux_z = factor_ref[:, 0:inner] * (field_ref[:, X:CELLS] - field_ref[:, 0:inner])
    proj_z = project(ph_ref, flux_z)
    xh, xl = halves(proj_x)
    yh, yl = halves(proj_y)
    less_x = (row == col).astype(F32) - ((within > 0) & (row == col - 1)).astype(F32)
    less_x = less_x.astype(BF16)
    less_y = ((row == col).astype(F32) - (row == col - COLS).astype(F32)).astype(BF16)
    for k in range(PLANES):
        lanes = slice(k * X, (k + 1) * X)
        owners = slice(k * OWNERS, (k + 1) * OWNERS)
        total = dot(xh[:, lanes], less_x) + dot(xl[:, lanes], less_x)
        total = total + dot(yh[:, lanes], less_y) + dot(yl[:, lanes], less_y)
        if k < PLANES - 1:
            total = total + proj_z[:, lanes]
        if k > 0:
            total = total - proj_z[:, (k - 1) * X : k * X]
        for m in range(OWN):
            modes = slice(m * OWNERS, (m + 1) * OWNERS)
            block_ref[owners, m, :] = total[modes]
            at = (m if m < 4 else 6 + m) * X
            edges[owners, at : at + X] = yh[modes, lanes]
            edges[owners, (4 + m) * X : (5 + m) * X] = xh[modes, lanes]
    back = (((1,), (1,)), ((), ()))
    block_ref[:, 6, :] = lax.dot_general(
        edges[:, 0 : 4 * X], columns[:, 0 : 4 * X], back, preferred_element_type=F32
    )
    block_ref[:, 7, :] = lax.dot_general(
        edges[:, 4 * X :], columns[:, 4 * X :], back, preferred_element_type=F32
    )


def join_kernel(
    upper_ref, lower_ref, vh_ref, vl_ref, ph_ref, factor_ref, field_ref, block_ref,
    out_ref,
    wide, above, faces, block,
):
    above[0:M] = upper_ref[...].astype(F32)
    wide[0 : 2 * M] = lower_ref[...].astype(F32)
    for m in range(OWN):
        modes = slice(m * OWNERS, (m + 1) * OWNERS)
        faces[modes, 0:X] = above[pl.ds(m, OWNERS, stride=OWN), :].astype(BF16)
        faces[modes, X : 2 * X] = wide[pl.ds(m, OWNERS, stride=2 * OWN), :].astype(BF16)
        faces[modes, 2 * X : 3 * X] = wide[pl.ds(OWN + m, OWNERS, stride=2 * OWN), :].astype(BF16)
    last = slice(CELLS - X, CELLS)
    values = dot(vh_ref[...], faces[...])
    top = factor_ref[:, last] * (values[:, 0:X] - field_ref[:, last])
    logs = values[:, X : 2 * X] + dot(vl_ref[...], faces[:, X : 2 * X])
    bottom = jnp.exp(logs) * (field_ref[:, 0:X] - values[:, 2 * X : 3 * X])
    both = project(ph_ref, jnp.concatenate([bottom, top], axis=1))
    block[...] = block_ref[...]
    for m in range(OWN):
        modes = slice(m * OWNERS, (m + 1) * OWNERS)
        block[0:OWNERS, m, :] -= both[modes, 0:X]
        block[3 * OWNERS : 4 * OWNERS, m, :] += both[modes, X : 2 * X]
    out_ref[...] = block[...].astype(BF16)


def finish_kernel(got_ref, source_ref, swap, shift, out_any, wide, ring, cells, ends, flat, planes, sems):
    wide[...] = got_ref[...].astype(F32)
    for b in range(ACROSS):
        lanes = slice(b * X, (b + 1) * X)
        for m in range(OWN):
            cells[m * DOWN : (m + 1) * DOWN, lanes] = wide[b, :, m, :].astype(BF16)
        cells[M : M + DOWN, lanes] = wide[b, :, 7, :].astype(BF16)
        for r in range(2):
            ring[1 : DOWN + 1, :] = wide[b, :, 6 + r, :]
            ring[0:1, :] = wide[b, DOWN - 1 : DOWN, 6 + r, :]
            at = M + (1 + r) * DOWN
            cells[at : at + DOWN, lanes] = ring[0:DOWN, :].astype(BF16)
    swapped = dot(cells[...], swap[...])
    for j in range(ROWS):
        ends[j * DOWN : (j + 1) * DOWN, :] = swapped[M : M + DOWN, j * X : (j + 1) * X].astype(BF16)
    beside = dot(ends[...], shift[...])
    above = swapped[M + DOWN : M + 2 * DOWN]
    halved = swapped[M + 2 * DOWN :]
    inside = lane_of(DOWN) % COLS < 16
    copies = []
    for m in range(OWN):
        modes = slice(m * DOWN, (m + 1) * DOWN)
        for j in range(ROWS):
            total = swapped[modes, j * X : (j + 1) * X]
            total = total - beside[j * DOWN : (j + 1) * DOWN, m * X : (m + 1) * X]
            if j == 0 and m < 4:
                total = total - above[:, m * X : (m + 1) * X]
            elif j == 0:
                at = 2 * (m - 4) * X
                far = turn(halved[:, at + X : at + 2 * X], 16)
                total = total - jnp.where(inside, halved[:, at : at + X], far)
            flat[pl.ds(j, DOWN, stride=ROWS), :] = total
        planes[m] = (-flat[0:X] - source_ref[m].astype(F32)).astype(BF16)
        copies.append(pltpu.make_async_copy(planes.at[m], out_any.at[m], sems.at[m]))
        copies[m].start()
    for copy in copies:
        copy.wait()


def call(kernel, outs, scratch, cost, **rest):
    outs = [jax.ShapeDtypeStruct(shape, dtype) for shape, dtype in outs]
    scratch = [pltpu.VMEM(*entry) if isinstance(entry, tuple) else entry for entry in scratch]
    return pl.pallas_call(
        kernel,
        out_shape=outs if len(outs) > 1 else outs[0],
        scratch_shapes=scratch,
        compiler_params=pltpu.CompilerParams(vmem_limit_bytes=VMEM),
        cost_estimate=pl.CostEstimate(flops=cost, bytes_accessed=2**20, transcendentals=0),
        **rest,
    )


def neighbour(block, distance):
    devices = range(lax.axis_size("x"))
    route = [((i - distance) % len(devices), i) for i in devices]
    return lax.ppermute(block, "x", route)


def exchange(block):
    return lax.all_to_all(block, ("y", "mode"), split_axis=0, concat_axis=0, tiled=True)


def shards(log_coeffs, pressure, source, vandermonde, weights):
    plane = (OWN, X, X)
    group = PLANES * OWNERS
    in_hbm = pl.BlockSpec(memory_space=pltpu.HBM)
    packed, points, past, swap, beside = call(
        pack_kernel,
        [
            ((group * SENT, X), BF16), ((1, Q), F32),
            ((X, 12 * X), BF16), ((4 * X, 4 * X), BF16), ((X, OWN * X), BF16),
        ],
        [
            ((2, *plane), BF16), ((X + 8, X), F32), ((DOWN + 8, X), F32),
            ((OWN * X, X), BF16), ((2 * M + 2 * DOWN, 4 * X), BF16),
            ((ACROSS * DOWN, OWN * X), BF16), ((group * SENT + 16, X), F32),
            pltpu.SemaphoreType.DMA((2, OWN)), pltpu.SemaphoreType.DMA,
        ],
        10**6,
        in_specs=[in_hbm] * 3,
    )(*[
        pltpu.with_memory_space_constraint(array, pltpu.HBM)
        for array in (log_coeffs.reshape(plane), pressure.reshape(plane), weights.reshape(1, Q))
    ])
    got = exchange(packed.reshape(group, SENT // 2, 2, X))
    upper = neighbour(got[0:OWNERS, 3:6], -1).reshape(M, X)
    lower = neighbour(got[group - OWNERS : group, 0:6], 1).reshape(2 * M, X)
    own = call(
        own_kernel,
        [
            ((Q, M), BF16), ((Q, M), BF16), ((M, Q), BF16),
            ((Q, CELLS), F32), ((Q, CELLS), F32), ((group, 8, X), F32),
        ],
        [
            ((group * SENT + 16, X), F32),
            ((M, CELLS), BF16), ((M, CELLS), BF16), ((M, CELLS), BF16), ((M, CELLS), BF16),
            ((OWN, group, X), BF16), ((2, group, X), BF16), ((group, 12 * X), BF16),
            ((M + 8, X), F32), ((M, Q), F32),
        ],
        10**9,
    )(got.reshape(group * SENT, X), vandermonde.T, points, past)
    back = call(
        join_kernel,
        [((group, 8, X), BF16)],
        [((2 * M + 16, X), F32), ((M + 8, X), F32), ((M, 3 * X), BF16), ((group, 8, X), F32)],
        10**9,
    )(upper, lower, *own)
    returned = exchange(back)
    result = call(
        finish_kernel,
        [(plane, BF16)],
        [
            ((ACROSS, DOWN, 8, X), F32), ((DOWN + 8, X), F32), ((M + 3 * DOWN, 4 * X), BF16),
            ((group, X), BF16), ((X + 8, X), F32), (plane, BF16), pltpu.SemaphoreType.DMA((OWN,)),
        ],
        10**6,
        out_specs=in_hbm,
    )(returned.reshape(ACROSS, DOWN, 8, X), source.reshape(plane), swap, beside)
    return result.reshape(OWN, 1, X, X)


def solution(mesh):
    grid = Mesh(mesh.devices.reshape(-1, PLANES, OWNERS), ("x", "y", "mode"))
    placed = P("mode", ("x", "y"), None, None)
    return jax.shard_map(
        shards, mesh=grid, in_specs=(placed, placed, placed, P(), P()), out_specs=placed, check_vma=False
    )
```

```python
import jax
import jax.numpy as jnp
from jax import lax
from jax.experimental import pallas as pl
from jax.experimental.pallas import tpu as pltpu
from jax.sharding import Mesh
from jax.sharding import PartitionSpec as P

F32 = jnp.float32
BF16 = jnp.bfloat16
OWN = 6
OWNERS = 32
M = OWN * OWNERS
Q = 512
X = 128
PLANES = 4
ROWS = 4
COLS = 32
ACROSS = 4
DOWN = 32
CELLS = PLANES * X
SENT = 14
VMEM = 48 * 1024 * 1024


def halves(values):
    high = values.astype(BF16)
    return high, (values - high.astype(F32)).astype(BF16)


def dot(a, b):
    return jnp.dot(a, b, preferred_element_type=F32)


def expand(vh_ref, vl_ref, field):
    return dot(vh_ref[...], field) + dot(vl_ref[...], field)


def project(ph_ref, flux):
    fh, fl = halves(flux)
    return dot(ph_ref[...], fh) + dot(ph_ref[...], fl)


def lane_of(rows):
    return lax.broadcasted_iota(jnp.int32, (rows, X), 1)


def turn(values, lanes):
    lanes = lanes % X
    return pltpu.roll(values, lanes, 1) if lanes else values


def grid_of(rows, columns):
    return tuple(lax.broadcasted_iota(jnp.int32, (rows, columns), axis) for axis in (0, 1))


def select(flags):
    return flags.astype(F32).astype(BF16)


def swapper():
    row, col = grid_of(4 * X, 4 * X)
    return select(row == col % X // COLS * X + col // X * COLS + col % COLS)


def start_all(copies):
    for copy in copies:
        copy.start()
    return copies


def fill_tables(past_ref, beside_ref):
    row, col = grid_of(X, X)
    within = col % COLS
    for m in range(4):
        past_ref[:, m * X : (m + 1) * X] = select((col >= 96) & (row == col - 96 + COLS * m))
    for m in range(OWN):
        at = (4 + m) * X
        past_ref[:, at : at + X] = select((within == COLS - 1) & (row == col - 5 + m))
    for m in range(4, OWN):
        at = (6 + m) * X
        half = jnp.where(col >= 112, 80, 96)
        past_ref[:, at : at + X] = select((col >= 96) & (row == col - half + 64 * (m - 4)))
    for m in range(OWN):
        here = select((within == 0) & (row == (col + X - COLS) % X + 26 + m))
        beside_ref[:, m * X : (m + 1) * X] = here


def fill_matrices(turned_ref, weights_ref, vh_ref, vl_ref, ph_ref, chunk, ordered):
    for c in range(Q // X):
        points = slice(c * X, (c + 1) * X)
        chunk[0:M] = turned_ref[:, points]
        for m in range(OWN):
            ordered[m * OWNERS : (m + 1) * OWNERS, points] = chunk[pl.ds(m, OWNERS, stride=OWN), :]
    vh_ref[...], vl_ref[...] = halves(jnp.transpose(ordered[...]))
    ph_ref[...] = (ordered[...] * weights_ref[...]).astype(BF16)


def pack_kernel(
    log_any, pressure_any, turned_any, weights_any,
    out_ref, vh_ref, vl_ref, ph_ref, past_ref, swap, beside_ref,
    planes, flat, ring, shift, cells, heads, block, turned, weights, chunk, ordered, sems, table_sems,
):
    copies = start_all([
        pltpu.make_async_copy(ref.at[m], planes.at[field, m], sems.at[field, m])
        for field, ref in enumerate((log_any, pressure_any))
        for m in range(OWN)
    ])
    tables = start_all([
        pltpu.make_async_copy(turned_any, turned, table_sems.at[0]),
        pltpu.make_async_copy(weights_any, weights, table_sems.at[1]),
    ])
    swap[...] = swapper()
    fill_tables(past_ref, beside_ref)
    row, col = grid_of(X, X)
    for m in range(OWN):
        shift[m * X : (m + 1) * X, :] = select((col % COLS == 26 + m) & (row == col - 26 - m))
    for field in range(2):
        for m in range(OWN):
            copies[field * OWN + m].wait()
            flat[0:X] = planes[field, m].astype(F32)
            rows = slice((field * OWN + m) * DOWN, (field * OWN + m + 1) * DOWN)
            for j in range(ROWS):
                cells[rows, j * X : (j + 1) * X] = flat[pl.ds(j, DOWN, stride=ROWS), :].astype(BF16)
            if field:
                ring[0:DOWN, :] = flat[pl.ds(0, DOWN, stride=ROWS), :]
                ring[DOWN : DOWN + 1, :] = flat[0:1, :]
                after = ring[1 : DOWN + 1, :]
                if m < 4:
                    cells[2 * M : 2 * M + DOWN, m * X : (m + 1) * X] = after.astype(BF16)
                else:
                    at = 2 * (m - 4) * X
                    cells[2 * M + DOWN :, at : at + X] = after.astype(BF16)
                    cells[2 * M + DOWN :, at + X : at + 2 * X] = turn(after, -16).astype(BF16)
    swapped = dot(cells[...], swap[...])
    for b in range(ACROSS):
        start = SENT * DOWN * b
        for field, offset in enumerate((0, OWN)):
            for m in range(OWN):
                rows = slice((field * OWN + m) * DOWN, (field * OWN + m + 1) * DOWN)
                total = swapped[rows, b * X : (b + 1) * X]
                block[pl.ds(start + offset + m, DOWN, stride=SENT), :] = total
                if field:
                    left = (b - 1) % ACROSS
                    heads[left * DOWN : (left + 1) * DOWN, m * X : (m + 1) * X] = total.astype(BF16)
        block[pl.ds(start + 12, DOWN, stride=SENT), :] = swapped[2 * M : 2 * M + DOWN, b * X : (b + 1) * X]
    rights = dot(heads[...], shift[...])
    within = lane_of(DOWN) % COLS
    for b in range(ACROSS):
        ends = swapped[2 * M + DOWN :, b * X : (b + 1) * X]
        total = jnp.where(within < 16, ends, rights[b * DOWN : (b + 1) * DOWN])
        block[pl.ds(SENT * DOWN * b + 13, DOWN, stride=SENT), :] = total
    out_ref[...] = block[0 : out_ref.shape[0]].astype(BF16)
    for copy in tables:
        copy.wait()
    fill_matrices(turned, weights, vh_ref, vl_ref, ph_ref, chunk, ordered)


def own_kernel(
    got_ref, vh_ref, vl_ref, ph_ref, columns,
    factor_ref, field_ref, block_ref,
    wide, logs, press, right, below, cells, ends, edges,
):
    row, col = grid_of(X, X)
    within = col % COLS
    wide[0 : got_ref.shape[0]] = got_ref[...].astype(F32)
    for k in range(PLANES):
        lanes = slice(k * X, (k + 1) * X)
        for r in range(2):
            ends[r, k * OWNERS : (k + 1) * OWNERS, :] = wide[
                pl.ds(SENT * OWNERS * k + 12 + r, OWNERS, stride=SENT), :
            ].astype(BF16)
        for m in range(OWN):
            modes = slice(m * OWNERS, (m + 1) * OWNERS)
            logs[modes, lanes] = wide[pl.ds(SENT * OWNERS * k + m, OWNERS, stride=SENT), :].astype(BF16)
            here = wide[pl.ds(SENT * OWNERS * k + 6 + m, OWNERS, stride=SENT), :].astype(BF16)
            press[modes, lanes] = here
            cells[m, k * OWNERS : (k + 1) * OWNERS, :] = here
    next_x = select((within < COLS - 1) & (row == col + 1))
    next_y = select(row == col + COLS)
    for m in range(OWN):
        modes = slice(m * OWNERS, (m + 1) * OWNERS)
        at = (4 + m) * X
        to_right = dot(cells[m], next_x) + dot(ends[1], columns[:, at : at + X])
        at = (m if m < 4 else 6 + m) * X
        to_below = dot(cells[m], next_y) + dot(ends[m // 4], columns[:, at : at + X])
        for k in range(PLANES):
            lanes = slice(k * X, (k + 1) * X)
            owners = slice(k * OWNERS, (k + 1) * OWNERS)
            right[modes, lanes] = to_right[owners].astype(BF16)
            below[modes, lanes] = to_below[owners].astype(BF16)
    factor_ref[...] = jnp.exp(expand(vh_ref, vl_ref, logs[...]))
    field_ref[...] = dot(vh_ref[...], press[...])
    flux_x = factor_ref[...] * (dot(vh_ref[...], right[...]) - field_ref[...])
    proj_x = project(ph_ref, flux_x)
    flux_y = factor_ref[...] * (dot(vh_ref[...], below[...]) - field_ref[...])
    proj_y = project(ph_ref, flux_y)
    inner = CELLS - X
    flux_z = factor_ref[:, 0:inner] * (field_ref[:, X:CELLS] - field_ref[:, 0:inner])
    proj_z = project(ph_ref, flux_z)
    xh, xl = halves(proj_x)
    yh, yl = halves(proj_y)
    less_x = (row == col).astype(F32) - ((within > 0) & (row == col - 1)).astype(F32)
    less_x = less_x.astype(BF16)
    less_y = ((row == col).astype(F32) - (row == col - COLS).astype(F32)).astype(BF16)
    for k in range(PLANES):
        lanes = slice(k * X, (k + 1) * X)
        owners = slice(k * OWNERS, (k + 1) * OWNERS)
        total = dot(xh[:, lanes], less_x) + dot(xl[:, lanes], less_x)
        total = total + dot(yh[:, lanes], less_y) + dot(yl[:, lanes], less_y)
        if k < PLANES - 1:
            total = total + proj_z[:, lanes]
        if k > 0:
            total = total - proj_z[:, (k - 1) * X : k * X]
        for m in range(OWN):
            modes = slice(m * OWNERS, (m + 1) * OWNERS)
            block_ref[owners, m, :] = total[modes]
            at = (m if m < 4 else 6 + m) * X
            edges[owners, at : at + X] = yh[modes, lanes]
            edges[owners, (4 + m) * X : (5 + m) * X] = xh[modes, lanes]
    back = (((1,), (1,)), ((), ()))
    block_ref[:, 6, :] = lax.dot_general(
        edges[:, 0 : 4 * X], columns[:, 0 : 4 * X], back, preferred_element_type=F32
    )
    block_ref[:, 7, :] = lax.dot_general(
        edges[:, 4 * X :], columns[:, 4 * X :], back, preferred_element_type=F32
    )


def join_kernel(
    upper_ref, lower_ref, vh_ref, vl_ref, ph_ref, factor_ref, field_ref, block_ref,
    out_ref,
    wide, above, faces, block,
):
    above[0:M] = upper_ref[...].astype(F32)
    wide[0 : 2 * M] = lower_ref[...].astype(F32)
    for m in range(OWN):
        modes = slice(m * OWNERS, (m + 1) * OWNERS)
        faces[modes, 0:X] = above[pl.ds(m, OWNERS, stride=OWN), :].astype(BF16)
        faces[modes, X : 2 * X] = wide[pl.ds(m, OWNERS, stride=2 * OWN), :].astype(BF16)
        faces[modes, 2 * X : 3 * X] = wide[pl.ds(OWN + m, OWNERS, stride=2 * OWN), :].astype(BF16)
    last = slice(CELLS - X, CELLS)
    values = dot(vh_ref[...], faces[...])
    top = factor_ref[:, last] * (values[:, 0:X] - field_ref[:, last])
    logs = values[:, X : 2 * X] + dot(vl_ref[...], faces[:, X : 2 * X])
    bottom = jnp.exp(logs) * (field_ref[:, 0:X] - values[:, 2 * X : 3 * X])
    both = project(ph_ref, jnp.concatenate([bottom, top], axis=1))
    outer = (slice(0, OWNERS), slice(3 * OWNERS, 4 * OWNERS))
    for rows in outer:
        block[rows] = block_ref[rows]
    out_ref[OWNERS : 3 * OWNERS] = block_ref[OWNERS : 3 * OWNERS].astype(BF16)
    for m in range(OWN):
        modes = slice(m * OWNERS, (m + 1) * OWNERS)
        block[0:OWNERS, m, :] -= both[modes, 0:X]
        block[3 * OWNERS : 4 * OWNERS, m, :] += both[modes, X : 2 * X]
    for rows in outer:
        out_ref[rows] = block[rows].astype(BF16)


def finish_kernel(got_ref, source_ref, swap, shift, out_any, wide, ring, cells, ends, flat, planes, sems):
    wide[...] = got_ref[...].astype(F32)
    for b in range(ACROSS):
        lanes = slice(b * X, (b + 1) * X)
        for m in range(OWN):
            cells[m * DOWN : (m + 1) * DOWN, lanes] = wide[b, :, m, :].astype(BF16)
        cells[M : M + DOWN, lanes] = wide[b, :, 7, :].astype(BF16)
        for r in range(2):
            ring[1 : DOWN + 1, :] = wide[b, :, 6 + r, :]
            ring[0:1, :] = wide[b, DOWN - 1 : DOWN, 6 + r, :]
            at = M + (1 + r) * DOWN
            cells[at : at + DOWN, lanes] = ring[0:DOWN, :].astype(BF16)
    swapped = dot(cells[...], swap[...])
    for j in range(ROWS):
        ends[j * DOWN : (j + 1) * DOWN, :] = swapped[M : M + DOWN, j * X : (j + 1) * X].astype(BF16)
    beside = dot(ends[...], shift[...])
    above = swapped[M + DOWN : M + 2 * DOWN]
    halved = swapped[M + 2 * DOWN :]
    inside = lane_of(DOWN) % COLS < 16
    copies = []
    for m in range(OWN):
        modes = slice(m * DOWN, (m + 1) * DOWN)
        for j in range(ROWS):
            total = swapped[modes, j * X : (j + 1) * X]
            total = total - beside[j * DOWN : (j + 1) * DOWN, m * X : (m + 1) * X]
            if j == 0 and m < 4:
                total = total - above[:, m * X : (m + 1) * X]
            elif j == 0:
                at = 2 * (m - 4) * X
                far = turn(halved[:, at + X : at + 2 * X], 16)
                total = total - jnp.where(inside, halved[:, at : at + X], far)
            flat[pl.ds(j, DOWN, stride=ROWS), :] = total
        planes[m] = (-flat[0:X] - source_ref[m].astype(F32)).astype(BF16)
        copies.append(pltpu.make_async_copy(planes.at[m], out_any.at[m], sems.at[m]))
        copies[m].start()
    for copy in copies:
        copy.wait()


def call(kernel, outs, scratch, cost, **rest):
    outs = [jax.ShapeDtypeStruct(shape, dtype) for shape, dtype in outs]
    scratch = [pltpu.VMEM(*entry) if isinstance(entry, tuple) else entry for entry in scratch]
    return pl.pallas_call(
        kernel,
        out_shape=outs if len(outs) > 1 else outs[0],
        scratch_shapes=scratch,
        compiler_params=pltpu.CompilerParams(vmem_limit_bytes=VMEM),
        cost_estimate=pl.CostEstimate(flops=cost, bytes_accessed=2**20, transcendentals=0),
        **rest,
    )


def neighbour(block, distance):
    devices = range(lax.axis_size("x"))
    route = [((i - distance) % len(devices), i) for i in devices]
    return lax.ppermute(block, "x", route)


def exchange(block):
    return lax.all_to_all(block, ("y", "mode"), split_axis=0, concat_axis=0, tiled=True)


def shards(log_coeffs, pressure, source, vandermonde, weights):
    plane = (OWN, X, X)
    group = PLANES * OWNERS
    in_hbm = pl.BlockSpec(memory_space=pltpu.HBM)
    packed, vh, vl, ph, past, swap, beside = call(
        pack_kernel,
        [
            ((group * SENT, X), BF16), ((Q, M), BF16), ((Q, M), BF16), ((M, Q), BF16),
            ((X, 12 * X), BF16), ((4 * X, 4 * X), BF16), ((X, OWN * X), BF16),
        ],
        [
            ((2, *plane), BF16), ((X + 8, X), F32), ((DOWN + 8, X), F32),
            ((OWN * X, X), BF16), ((2 * M + 2 * DOWN, 4 * X), BF16),
            ((ACROSS * DOWN, OWN * X), BF16), ((group * SENT + 16, X), F32),
            ((M, Q), F32), ((1, Q), F32), ((M + 8, X), F32), ((M, Q), F32),
            pltpu.SemaphoreType.DMA((2, OWN)), pltpu.SemaphoreType.DMA((2,)),
        ],
        10**6,
        in_specs=[in_hbm] * 4,
    )(*[
        pltpu.with_memory_space_constraint(array, pltpu.HBM)
        for array in (
            log_coeffs.reshape(plane), pressure.reshape(plane), vandermonde.T, weights.reshape(1, Q)
        )
    ])
    halved = (vh, vl, ph)
    got = exchange(packed.reshape(group, SENT // 2, 2, X))
    upper = neighbour(got[0:OWNERS, 3:6], -1).reshape(M, X)
    lower = neighbour(got[group - OWNERS : group, 0:6], 1).reshape(2 * M, X)
    own = call(
        own_kernel,
        [((Q, CELLS), F32), ((Q, CELLS), F32), ((group, 8, X), F32)],
        [
            ((group * SENT + 16, X), F32),
            ((M, CELLS), BF16), ((M, CELLS), BF16), ((M, CELLS), BF16), ((M, CELLS), BF16),
            ((OWN, group, X), BF16), ((2, group, X), BF16), ((group, 12 * X), BF16),
        ],
        10**9,
    )(got.reshape(group * SENT, X), *halved, past)
    back = call(
        join_kernel,
        [((group, 8, X), BF16)],
        [((2 * M + 16, X), F32), ((M + 8, X), F32), ((M, 3 * X), BF16), ((group, 8, X), F32)],
        10**9,
    )(upper, lower, *halved, *own)
    returned = exchange(back)
    result = call(
        finish_kernel,
        [(plane, BF16)],
        [
            ((ACROSS, DOWN, 8, X), F32), ((DOWN + 8, X), F32), ((M + 3 * DOWN, 4 * X), BF16),
            ((group, X), BF16), ((X + 8, X), F32), (plane, BF16), pltpu.SemaphoreType.DMA((OWN,)),
        ],
        10**6,
        out_specs=in_hbm,
    )(returned.reshape(ACROSS, DOWN, 8, X), source.reshape(plane), swap, beside)
    return result.reshape(OWN, 1, X, X)


def solution(mesh):
    grid = Mesh(mesh.devices.reshape(-1, PLANES, OWNERS), ("x", "y", "mode"))
    placed = P("mode", ("x", "y"), None, None)
    return jax.shard_map(
        shards, mesh=grid, in_specs=(placed, placed, placed, P(), P()), out_specs=placed, check_vma=False
    )
```
